32 devices in a mesh: seq: 8 (over z, core), tensor: 4 (over y, x).
Axes of the slice: x: 2, y: 2, z: 4, core: 2. Of those that a mesh axis runs over, the one named last changes fastest.
Arguments:
- tokens: bfloat16 [2, 1024, 3072], P(None, 'seq'), as said below
- w_query: bfloat16 [3072, 3072], P(None, 'tensor'), as said below
- w_key: bfloat16 [3072, 3072], P(None, 'tensor'), as said below
- w_value: bfloat16 [3072, 3072], P(None, 'tensor'), as said below
- w_out: bfloat16 [3072, 3072], P('tensor'), as said below
- cotangent: bfloat16 [2, 1024, 3072], P(None, 'seq'), may hold values from -6 to 6
- noise_value: float32 [3072, 3072], P('seq', 'tensor'), may hold values from -6 to 6
- noise_out: float32 [3072, 3072], P('tensor', 'seq'), may hold values from -6 to 6
Outputs:
- grad_value: float32 [3072, 3072], P('seq', 'tensor')
- grad_out: float32 [3072, 3072], P('tensor', 'seq')
The draws below stay inside these ranges and needn't reach their ends.
Inputs may be any that keep to these rules, and one draw needn't show every extreme that they name: `tokens`: patch activations. `w_query`: scaled by the fan-in. `w_key`: scaled by the fan-in. `w_value`: scaled by the fan-in. `w_out`: scaled by the fan-in.
All inputs are finite; a program needn't handle non-finite values.
Results may differ from the reference program's by a relative error of at most 0.023.
Values may be sent and summed in bfloat16 or wider, within the bound.
A program may use at most 128 MiB of HBM per device.

```python
import math
import jax
import jax.numpy as jnp
from jax import lax

D = 3072
HEADS = 24
HEAD_DIM = 128
IMGS = 2
PATCH_DEV = 128
PATCHES = 1024
N_SEQ = 8


def shared_query(key):
    return jax.random.normal(key, (D, HEADS * HEAD_DIM), jnp.float32)


def head_scales(key, repeat):
    rising = 1.0 + 2.0 * jnp.arange(HEADS, dtype=jnp.float32) / HEADS
    rough = jnp.exp(jax.random.uniform(key, (HEADS,), jnp.float32, 0.0, math.log(2.0)))
    return jnp.repeat(rising * rough, repeat) / 2.2


def draw_tokens(key, part):
    key = jax.random.fold_in(key, 11)
    key_one, key_two = jax.random.split(key, 2)
    rising = 1.0 + 2.0 * jnp.arange(D, dtype=jnp.float32) / D
    feature = rising * jnp.exp(jax.random.uniform(key_one, (D,), jnp.float32, 0.0, math.log(4.0))) / 5.0
    normal_base = jnp.clip(jax.random.normal(key_two, (IMGS, PATCHES, D), jnp.float32), -6.0, 6.0)
    values = normal_base * feature
    return values.astype(jnp.bfloat16)


def draw_w_query(key, part):
    shared = shared_query(key)
    return (jnp.clip(shared, -5.0, 5.0) / math.sqrt(D)).astype(jnp.bfloat16)


def draw_w_key(key, part):
    key = jax.random.fold_in(key, 13)
    fresh_part = jax.random.normal(key, (D, HEADS * HEAD_DIM), jnp.float32)
    blended = fresh_part
    return (jnp.clip(blended, -5.0, 5.0) / math.sqrt(D)).astype(jnp.bfloat16)


def draw_w_value(key, part):
    key = jax.random.fold_in(key, 14)
    key_one, key_two = jax.random.split(key)
    columns = head_scales(key_one, HEAD_DIM)
    normal_base = jnp.clip(jax.random.normal(key_two, (D, HEADS * HEAD_DIM), jnp.float32), -5.0, 5.0)
    return (normal_base * columns[None, :] / math.sqrt(D)).astype(jnp.bfloat16)


def draw_w_out(key, part):
    key = jax.random.fold_in(key, 15)
    key_one, key_two = jax.random.split(key)
    row_scale = head_scales(key_one, HEAD_DIM)
    normal_base = jnp.clip(jax.random.normal(key_two, (HEADS * HEAD_DIM, D), jnp.float32), -5.0, 5.0)
    return (normal_base * row_scale[:, None] / math.sqrt(HEADS * HEAD_DIM)).astype(jnp.bfloat16)


def levels(key, dims, shards, low, top_value):
    loudness, own = 1.0, jax.random.fold_in(key, 6)
    for axis_at, blocks in shards:
        steps = jnp.exp(jax.random.uniform(jax.random.fold_in(own, axis_at), (blocks,), jnp.float32, low / len(shards), top_value / len(shards)))
        loudness = loudness * jnp.repeat(steps, dims[axis_at] // blocks).reshape([-1 if axis == axis_at else 1 for axis in range(len(dims))])
    return loudness


def centred(own_key, shape, spread, bound, shards=(), held_as=jnp.bfloat16):
    entries = jax.random.normal(own_key, shape, jnp.float32) * spread
    if len(shards) > 0:
        entries = levels(own_key, shape, shards, -0.22, 0.18) * entries
    return jnp.clip(entries, min=-bound, max=bound).astype(held_as)


def setup_inputs(seed: int = 0) -> dict:
    key_of = jax.random.split(jax.random.key(seed), 9)
    tokens = draw_tokens(jax.random.fold_in(key_of[8], 71), 0)
    w_query = draw_w_query(jax.random.fold_in(key_of[8], 71), 0)
    w_key = draw_w_key(jax.random.fold_in(key_of[8], 71), 0)
    w_value = draw_w_value(jax.random.fold_in(key_of[8], 71), 0)
    w_out = draw_w_out(jax.random.fold_in(key_of[8], 71), 0)
    cotangent = centred(key_of[5], (IMGS, PATCHES, D), 1.0, 6.0, ((1, 8),))
    noise_value = centred(key_of[6], (D, HEADS * HEAD_DIM), 1.0, 6.0, ((0, 8), (1, 4)), jnp.float32)
    noise_out = centred(key_of[7], (HEADS * HEAD_DIM, D), 1.0, 6.0, ((0, 4), (1, 8)), jnp.float32)
    return {"tokens": tokens, "w_query": w_query, "w_key": w_key, "w_value": w_value, "w_out": w_out, "cotangent": cotangent, "noise_value": noise_value, "noise_out": noise_out}


def project_rows(tokens, weight):
    flat_tokens = tokens.reshape(-1, tokens.shape[-1])
    return jnp.dot(flat_tokens, weight, preferred_element_type=jnp.float32).astype(jnp.bfloat16)

def block_product(left_side, right_side):
    left_blocks = left_side.reshape(N_SEQ, PATCH_DEV, left_side.shape[-1])
    right_blocks = right_side.reshape(N_SEQ, PATCH_DEV, right_side.shape[-1])

    def add_block(running, block_pair):
        product = jnp.dot(block_pair[0].T, block_pair[1], preferred_element_type=jnp.float32)
        rounded = lax.optimization_barrier(product.astype(jnp.bfloat16))
        return (running + rounded.astype(jnp.float32), None)
    initial = jnp.zeros((left_side.shape[-1], right_side.shape[-1]), jnp.float32)
    return lax.scan(add_block, initial, (left_blocks, right_blocks))[0]

def heads_first(array):
    return array.reshape(IMGS, PATCHES, HEADS, HEAD_DIM).transpose(0, 2, 1, 3).reshape(IMGS * HEADS, PATCHES, HEAD_DIM)

def heads_last(array):
    return array.reshape(IMGS, HEADS, PATCHES, HEAD_DIM).transpose(0, 2, 1, 3).reshape(IMGS, PATCHES, HEADS * HEAD_DIM)

def reference(tokens, w_query, w_key, w_value, w_out, cotangent, noise_value, noise_out):
    score_scale = 1.0 / math.sqrt(HEAD_DIM)
    queries = heads_first(project_rows(tokens, w_query))
    keys_full = heads_first(project_rows(tokens, w_key))
    values_full = heads_first(project_rows(tokens, w_value))
    d_attn = jnp.dot(cotangent.reshape(-1, D), w_out.T, preferred_element_type=jnp.float32).astype(jnp.bfloat16)
    d_attn = heads_first(d_attn)

    def per_head(head_items):
        query_head, key_head, value_head, grad_head = head_items
        scores = jnp.dot(query_head, key_head.T, preferred_element_type=jnp.float32) * score_scale
        row_totals = jax.nn.logsumexp(scores, axis=1, keepdims=True)
        attn_probs = jnp.exp(scores - row_totals).astype(jnp.bfloat16)
        attended = jnp.dot(attn_probs, value_head, preferred_element_type=jnp.float32).astype(jnp.bfloat16)
        d_value = block_product(attn_probs, grad_head).astype(jnp.bfloat16)
        return (attended, d_value)
    attended, d_value = lax.map(per_head, (queries, keys_full, values_full, d_attn))
    attended = heads_last(attended)
    d_value = heads_last(d_value)
    per_value = []
    per_out = []
    for image_index in range(IMGS):
        per_value.append(block_product(tokens[image_index], d_value[image_index]))
        per_out.append(block_product(attended[image_index], cotangent[image_index]))
    clip_bound = math.sqrt(2.0 * D * HEADS * HEAD_DIM)
    grad_value = noise_value
    grad_out = noise_out
    for image_index in range(IMGS):
        squares = jnp.sum(jnp.square(per_value[image_index])) + jnp.sum(jnp.square(per_out[image_index]))
        factor = clip_bound / (jnp.sqrt(squares) + 0.01)
        grad_value = grad_value + factor * per_value[image_index]
        grad_out = grad_out + factor * per_out[image_index]
    return (grad_value / IMGS, grad_out / IMGS)
```

```python
import math

import jax
import jax.numpy as jnp
from jax import lax
from jax.sharding import PartitionSpec as P

HEAD_DIM = 128


def local(tokens, w_query, w_key, w_value, w_out, cotangent, noise_value, noise_out):
    images, patch_rows, width = tokens.shape
    columns = w_query.shape[1]
    head_count = columns // HEAD_DIM
    score_scale = 1.0 / math.sqrt(HEAD_DIM)
    clip_bound = math.sqrt(2.0 * width * width)
    flat_tokens = tokens.reshape(images * patch_rows, width)

    token_columns = lax.all_to_all(tokens, "seq", split_axis=2, concat_axis=1, tiled=True)
    cot_columns = lax.all_to_all(cotangent, "seq", split_axis=2, concat_axis=1, tiled=True)

    def heads_first(rows):
        split = rows.reshape(images, patch_rows, head_count, HEAD_DIM)
        return split.transpose(0, 2, 1, 3)

    def project(weight):
        product = jnp.dot(flat_tokens, weight, preferred_element_type=jnp.float32)
        return product.astype(jnp.bfloat16)

    key_local = heads_first(project(w_key))
    keys_all = lax.all_gather(key_local, "seq", axis=2, tiled=True)
    value_local = heads_first(project(w_value))
    values_all = lax.all_gather(value_local, "seq", axis=2, tiled=True)
    queries = heads_first(project(w_query))
    flat_cotangent = cotangent.reshape(images * patch_rows, width)
    d_attn = jnp.einsum("rd,cd->rc", flat_cotangent, w_out, preferred_element_type=jnp.float32)
    d_attn = heads_first(d_attn.astype(jnp.bfloat16))
    scores = (
        jnp.einsum("ihqd,ihkd->ihqk", queries, keys_all, preferred_element_type=jnp.float32)
        * score_scale
    )
    row_totals = jax.nn.logsumexp(scores, axis=-1)
    attn_probs = jnp.exp(scores - row_totals[..., None]).astype(jnp.bfloat16)
    d_value = jnp.einsum(
        "ihqk,ihqd->ihkd", attn_probs, d_attn, preferred_element_type=jnp.float32
    ).astype(jnp.bfloat16)
    d_value = lax.psum_scatter(d_value, "seq", scatter_dimension=2, tiled=True)
    d_value_all = lax.all_gather(d_value, "seq", axis=2, tiled=True)
    attended = jnp.einsum(
        "ihqk,ihkd->ihqd", attn_probs, values_all, preferred_element_type=jnp.float32
    ).astype(jnp.bfloat16)
    attended_all = lax.all_gather(attended, "seq", axis=2, tiled=True)

    per_value = jnp.einsum(
        "ipe,ihpd->iehd", token_columns, d_value_all, preferred_element_type=jnp.float32
    ).reshape(images, -1, columns)
    per_out = jnp.einsum(
        "ihpd,ipe->ihde", attended_all, cot_columns, preferred_element_type=jnp.float32
    ).reshape(images, columns, -1)
    partial = jnp.sum(jnp.square(per_value), axis=(1, 2)) + jnp.sum(jnp.square(per_out), axis=(1, 2))
    squares = lax.psum(partial, ("seq", "tensor"))
    factor = clip_bound / (jnp.sqrt(squares) + 0.01)
    grad_value = noise_value
    grad_out = noise_out
    for image_index in range(images):
        grad_value = grad_value + factor[image_index] * per_value[image_index]
        grad_out = grad_out + factor[image_index] * per_out[image_index]
    return (grad_value / images, grad_out / images)


def solution(mesh):
    placed = (
        P(None, "seq", None),
        P(None, "tensor"),
        P(None, "tensor"),
        P(None, "tensor"),
        P("tensor", None),
        P(None, "seq", None),
        P("seq", "tensor"),
        P("tensor", "seq"),
    )
    return jax.shard_map(
        local,
        mesh=mesh,
        in_specs=placed,
        out_specs=(P("seq", "tensor"), P("tensor", "seq")),
        check_vma=False,
    )
```

```python
import functools
import math

import jax
import jax.numpy as jnp
from jax import lax
from jax.experimental import pallas as pl
from jax.experimental.pallas import tpu as pltpu
from jax.sharding import PartitionSpec as P

HEAD_DIM = 128


def local_general(tokens, w_query, w_key, w_value, w_out, cotangent, noise_value, noise_out):
    images, patch_rows, width = tokens.shape
    columns = w_query.shape[1]
    head_count = columns // HEAD_DIM
    score_scale = 1.0 / math.sqrt(HEAD_DIM)
    clip_bound = math.sqrt(2.0 * width * width)
    flat_tokens = tokens.reshape(images * patch_rows, width)

    token_columns = lax.all_to_all(tokens, "seq", split_axis=2, concat_axis=1, tiled=True)
    cot_columns = lax.all_to_all(cotangent, "seq", split_axis=2, concat_axis=1, tiled=True)

    def heads_first(rows):
        split = rows.reshape(images, patch_rows, head_count, HEAD_DIM)
        return split.transpose(0, 2, 1, 3)

    def project(weight):
        product = jnp.dot(flat_tokens, weight, preferred_element_type=jnp.float32)
        return product.astype(jnp.bfloat16)

    key_local = heads_first(project(w_key))
    keys_all = lax.all_gather(key_local, "seq", axis=2, tiled=True)
    value_local = heads_first(project(w_value))
    values_all = lax.all_gather(value_local, "seq", axis=2, tiled=True)
    queries = heads_first(project(w_query))
    flat_cotangent = cotangent.reshape(images * patch_rows, width)
    d_attn = jnp.einsum("rd,cd->rc", flat_cotangent, w_out, preferred_element_type=jnp.float32)
    d_attn = heads_first(d_attn.astype(jnp.bfloat16))
    scores = (
        jnp.einsum("ihqd,ihkd->ihqk", queries, keys_all, preferred_element_type=jnp.float32)
        * score_scale
    )
    row_totals = jax.nn.logsumexp(scores, axis=-1)
    attn_probs = jnp.exp(scores - row_totals[..., None]).astype(jnp.bfloat16)
    d_value = jnp.einsum(
        "ihqk,ihqd->ihkd", attn_probs, d_attn, preferred_element_type=jnp.float32
    ).astype(jnp.bfloat16)
    d_value = lax.psum_scatter(d_value, "seq", scatter_dimension=2, tiled=True)
    d_value_all = lax.all_gather(d_value, "seq", axis=2, tiled=True)
    attended = jnp.einsum(
        "ihqk,ihkd->ihqd", attn_probs, values_all, preferred_element_type=jnp.float32
    ).astype(jnp.bfloat16)
    attended_all = lax.all_gather(attended, "seq", axis=2, tiled=True)

    per_value = jnp.einsum(
        "ipe,ihpd->iehd", token_columns, d_value_all, preferred_element_type=jnp.float32
    ).reshape(images, -1, columns)
    per_out = jnp.einsum(
        "ihpd,ipe->ihde", attended_all, cot_columns, preferred_element_type=jnp.float32
    ).reshape(images, columns, -1)
    partial = jnp.sum(jnp.square(per_value), axis=(1, 2)) + jnp.sum(jnp.square(per_out), axis=(1, 2))
    squares = lax.psum(partial, ("seq", "tensor"))
    factor = clip_bound / (jnp.sqrt(squares) + 0.01)
    grad_value = noise_value
    grad_out = noise_out
    for image_index in range(images):
        grad_value = grad_value + factor[image_index] * per_value[image_index]
        grad_out = grad_out + factor[image_index] * per_out[image_index]
    return (grad_value / images, grad_out / images)


MESH = pl.DeviceIdType.MESH
F32 = jnp.float32
BF16 = jnp.bfloat16
ROWS_DOT = (((1,), (1,)), ((), ()))
DEPTH_DOT = (((0,), (0,)), ((), ()))


def fused_kernel(
    n_seq, n_ten, tok_h, cot_h, wq_h, wk_h, wv_h, wo_h, nv_h, no_h, gv, go,
    tok, cot, w3, wo, loc, recv, tmp, gath, cols, cols_t, acc, nv, no, dv_t, sq_seq, sq_ten,
    in_sem, w_sem, own_sem, a2a_s, a2a_r, tk_s, tk_r, fw_s, fw_r,
    ag_s, ag_r, sib_s, sib_r, sq_s, sq_r, st_s, st_r,
):
    me = lax.axis_index("seq")
    ten = lax.axis_index("tensor")
    chip, core = me // 2, me % 2
    n_chip = n_seq // 2
    sibling = 2 * chip + 1 - core
    rows = tok.shape[0]
    patch = rows // 2
    width = tok.shape[1]
    block = width // n_seq
    quarter = rows // n_ten
    patches = patch * n_seq
    half = patches // 2
    score_scale = 1.0 / math.sqrt(HEAD_DIM)

    loads = [
        pltpu.make_async_copy(tok_h, tok, in_sem.at[0]),
        pltpu.make_async_copy(wk_h, w3.at[0], w_sem.at[0]),
        pltpu.make_async_copy(wq_h, w3.at[1], w_sem.at[1]),
        pltpu.make_async_copy(wv_h, w3.at[2], w_sem.at[2]),
        pltpu.make_async_copy(cot_h, cot, in_sem.at[1]),
        pltpu.make_async_copy(wo_h, wo, w_sem.at[3]),
        pltpu.make_async_copy(nv_h, nv, in_sem.at[2]),
        pltpu.make_async_copy(no_h, no, in_sem.at[3]),
    ]
    for load in loads:
        load.start()

    barrier = pltpu.get_barrier_semaphore()
    for step in range(1, n_seq):
        pl.semaphore_signal(
            barrier, inc=1, device_id=((me + step) % n_seq, ten), device_id_type=MESH
        )
    for step in range(1, n_ten):
        pl.semaphore_signal(
            barrier, inc=1, device_id=(me, (ten + step) % n_ten), device_id_type=MESH
        )
    pl.semaphore_wait(barrier, n_seq + n_ten - 2)

    def remote(source, target, send_sem, recv_sem, seq_at, ten_at):
        return pltpu.make_async_remote_copy(
            src_ref=source, dst_ref=target, send_sem=send_sem, recv_sem=recv_sem,
            device_id=(seq_at, ten_at), device_id_type=MESH,
        )

    def first_head(device):
        return 3 * ((device // 2) % 2) + device % 2

    def image_of(device):
        return device // 4

    def head_rows(device):
        return pl.ds(pl.multiple_of(device * patch, patch), patch)

    def exchange(kind, step, source):
        peer = (me + step) % n_seq
        if source:
            peer = (me + n_seq - step) % n_seq
        sender, target = (peer, me) if source else (me, peer)
        return remote(
            loc.at[kind, pl.ds(first_head(target), 2),
                   pl.ds(pl.multiple_of(image_of(target) * patch, patch), patch)],
            recv.at[kind, :, head_rows(sender)],
            a2a_s.at[kind, step], a2a_r.at[kind, step], peer, ten,
        )

    def send_heads(kind):
        @pl.loop(1, n_seq)
        def _(step):
            exchange(kind, step, False).start()

        recv[kind, :, head_rows(me), :] = loc[
            kind, pl.ds(first_head(me), 2),
            pl.ds(pl.multiple_of(image_of(me) * patch, patch), patch), :
        ]

    def project(kind):
        @pl.loop(0, 3)
        def _(at):
            chunk = pl.ds(pl.multiple_of(at * 256, 256), 256)
            if kind < 3:
                out = jnp.dot(tok[...], w3[kind, :, chunk], preferred_element_type=F32)
            else:
                out = lax.dot_general(cot[...], wo[chunk, :], ROWS_DOT, preferred_element_type=F32)
            out = out.astype(BF16)
            loc[kind, 2 * at] = out[:, :HEAD_DIM]
            loc[kind, 2 * at + 1] = out[:, HEAD_DIM:]

    loads[0].wait()
    for kind in range(3):
        loads[1 + kind].wait()
        project(kind)
        send_heads(kind)
    loads[4].wait()
    loads[5].wait()
    project(3)
    send_heads(3)

    held = (tok, cot)

    def own_columns(which):
        return pltpu.make_async_copy(
            held[which].at[:, pl.ds(pl.multiple_of(me * block, block), block)],
            cols.at[which, me], own_sem.at[which],
        )

    def ten_rows(index):
        return pl.ds(pl.multiple_of(index * quarter, quarter), quarter)

    def column_copy(which, step, source):
        peer = (me + step) % n_seq
        if source:
            peer = (me + n_seq - step) % n_seq
        sender, target = (peer, me) if source else (me, peer)
        return remote(
            held[which].at[ten_rows(ten), pl.ds(pl.multiple_of(target * block, block), block)],
            cols.at[which, sender, ten_rows(ten), :],
            tk_s.at[which, step], tk_r.at[which, step], peer, ten,
        )

    def column_share(which, step, hop, source):
        origin = (me + n_seq - step) % n_seq
        peer = (ten + hop) % n_ten
        if source:
            peer = (ten + n_ten - hop) % n_ten
        piece = cols.at[which, origin, ten_rows(peer if source else ten), :]
        return remote(
            piece, piece, fw_s.at[which, step, hop], fw_r.at[which, step, hop], me, peer
        )

    for which in range(2):
        own_columns(which).start()

        @pl.loop(1, n_seq)
        def _(step):
            column_copy(which, step, False).start()

    for kind in range(4):
        @pl.loop(1, n_seq)
        def _(step):
            exchange(kind, step, True).wait_recv()

    @pl.loop(0, 2)
    def _(slot):
        dv_t[...] = jnp.zeros_like(dv_t)

        @pl.loop(0, patches // 256)
        def _(at):
            part = pl.ds(pl.multiple_of(at * 256, 256), 256)
            scores = lax.dot_general(
                recv[1, slot, part, :], recv[0, slot], ROWS_DOT, preferred_element_type=F32
            ) * score_scale
            top = jnp.max(scores, axis=1, keepdims=True)
            raised = jnp.exp(scores - top)
            total = jnp.sum(raised, axis=1, keepdims=True)
            probs = (raised * (1.0 / total)).astype(BF16)
            attended = jnp.dot(probs, recv[2, slot], preferred_element_type=F32)
            tmp[0, slot, part, :] = attended.astype(BF16)
            dv_t[...] += lax.dot_general(
                recv[3, slot, part, :], probs, DEPTH_DOT, preferred_element_type=F32
            )

        tmp[1, slot] = dv_t[...].T.astype(BF16)

    def own_head(at_chip, at_core):
        return (at_chip // 2) * 6 + 3 * (at_chip % 2) + 2 * at_core

    def shared_head(at_chip):
        return (at_chip // 2) * 6 + 3 * (at_chip % 2) + 1

    def half_rows(at_core):
        return pl.ds(pl.multiple_of(at_core * half, half), half)

    def place(which, part, at_chip, at_core):
        if part == 0:
            return gath.at[which, own_head(at_chip, at_core)]
        return gath.at[which, shared_head(at_chip), half_rows(at_core), :]

    def made(which, part):
        if part == 0:
            return tmp.at[which, core]
        return tmp.at[which, 1 - core, half_rows(core), :]

    def plane_copy(which, part, step, source):
        other = (chip + step) % n_chip
        if source:
            other = (chip + n_chip - step) % n_chip
        return remote(
            made(which, part), place(which, part, other if source else chip, core),
            ag_s.at[which, part, step], ag_r.at[which, part, step], 2 * other + core, ten,
        )

    def sibling_copy(which, part, step, source):
        origin = (chip + n_chip - step) % n_chip
        piece = place(which, part, origin, 1 - core if source else core)
        return remote(
            piece, piece, sib_s.at[which, part, step], sib_r.at[which, part, step], sibling, ten
        )

    for which in range(2):
        for part in range(2):
            @pl.loop(1, n_chip)
            def _(step):
                plane_copy(which, part, step, False).start()

        gath[which, own_head(chip, core)] = tmp[which, core]
        gath[which, shared_head(chip), half_rows(core), :] = tmp[
            which, 1 - core, half_rows(core), :
        ]
        for part in range(2):
            sibling_copy(which, part, 0, False).start()

    for which in range(2):
        @pl.loop(1, n_seq)
        def _(step):
            column_copy(which, step, True).wait_recv()

            @pl.loop(1, n_ten)
            def _(hop):
                column_share(which, step, hop, False).start()

        own_columns(which).wait()

    for which in range(2):
        @pl.loop(1, n_seq)
        def _(step):
            @pl.loop(1, n_ten)
            def _(hop):
                column_share(which, step, hop, True).wait_recv()

        @pl.loop(0, n_seq)
        def _(origin):
            lanes = pl.ds(pl.multiple_of(origin * patch, patch), patch)
            for image in range(2):
                piece = cols[which, origin, image * patch:(image + 1) * patch, :]
                cols_t[which, image, :, lanes] = piece.T

    for which in range(2):
        @pl.loop(1, n_chip)
        def _(step):
            for part in range(2):
                plane_copy(which, part, step, True).wait_recv()
                sibling_copy(which, part, step, False).start()

    squares = [jnp.zeros((1, 256), F32), jnp.zeros((1, 256), F32)]
    for which in range(2):
        @pl.loop(0, n_chip)
        def _(step):
            for part in range(2):
                sibling_copy(which, part, step, True).wait_recv()

        for image in range(2):
            for at in range(3):
                head = image * 6 + 2 * at
                heads = jnp.concatenate([gath[which, head], gath[which, head + 1]], axis=1)
                product = jnp.dot(
                    cols_t[1 - which, image], heads, preferred_element_type=F32
                )
                acc[which, image, :, at * 256:(at + 1) * 256] = product
                squares[image] += jnp.sum(product * product, axis=0, keepdims=True)

    def spread(value):
        return jnp.broadcast_to(jnp.sum(value, axis=1, keepdims=True), (8, HEAD_DIM))

    sq_seq[me, 0:8, :] = spread(squares[0])
    sq_seq[me, 8:16, :] = spread(squares[1])

    def square_seq(step, source):
        peer = (me + step) % n_seq
        if source:
            peer = (me + n_seq - step) % n_seq
        piece = sq_seq.at[peer if source else me]
        return remote(piece, piece, sq_s.at[step], sq_r.at[step], peer, ten)

    def square_ten(step, source):
        peer = (ten + step) % n_ten
        if source:
            peer = (ten + n_ten - step) % n_ten
        piece = sq_ten.at[peer if source else ten]
        return remote(piece, piece, st_s.at[step], st_r.at[step], me, peer)

    for step in range(1, n_seq):
        square_seq(step, False).start()
    for step in range(1, n_seq):
        square_seq(step, True).wait_recv()
    sq_ten[ten] = jnp.sum(sq_seq[...], axis=0)
    for step in range(1, n_ten):
        square_ten(step, False).start()
    loads[6].wait()
    loads[7].wait()
    for step in range(1, n_ten):
        square_ten(step, True).wait_recv()
    norm = jnp.sum(sq_ten[...], axis=0)
    factor = math.sqrt(2.0 * width * width) / (jnp.sqrt(norm) + 0.01)
    first, second = factor[0:1, 0:1], factor[8:9, 0:1]

    @pl.loop(0, 6)
    def _(at):
        lanes = pl.ds(pl.multiple_of(at * HEAD_DIM, HEAD_DIM), HEAD_DIM)
        value = nv[:, lanes] + first * acc[1, 0, :, lanes] + second * acc[1, 1, :, lanes]
        gv[:, lanes] = value * 0.5
        mixed = first * acc[0, 0, :, lanes] + second * acc[0, 1, :, lanes]
        go[lanes, :] = (no[lanes, :] + mixed.T) * 0.5

    for kind in range(4):
        @pl.loop(1, n_seq)
        def _(step):
            exchange(kind, step, False).wait_send()
    for which in range(2):
        @pl.loop(1, n_seq)
        def _(step):
            column_copy(which, step, False).wait_send()

            @pl.loop(1, n_ten)
            def _(hop):
                column_share(which, step, hop, False).wait_send()

        for part in range(2):
            @pl.loop(1, n_chip)
            def _(step):
                plane_copy(which, part, step, False).wait_send()

            @pl.loop(0, n_chip)
            def _(step):
                sibling_copy(which, part, step, False).wait_send()
    for step in range(1, n_seq):
        square_seq(step, False).wait_send()
    for step in range(1, n_ten):
        square_ten(step, False).wait_send()


def local_fused(
    n_seq, n_ten, tokens, w_query, w_key, w_value, w_out, cotangent, noise_value, noise_out
):
    images, patch, width = tokens.shape
    columns = w_query.shape[1]
    rows, patches, block = images * patch, patch * n_seq, width // n_seq
    n_chip = n_seq // 2
    dma = pltpu.SemaphoreType.DMA
    return pl.pallas_call(
        functools.partial(fused_kernel, n_seq, n_ten),
        out_shape=(
            jax.ShapeDtypeStruct(noise_value.shape, F32),
            jax.ShapeDtypeStruct(noise_out.shape, F32),
        ),
        in_specs=[pl.BlockSpec(memory_space=pl.ANY)] * 8,
        out_specs=[pl.BlockSpec(memory_space=pltpu.VMEM)] * 2,
        scratch_shapes=[
            pltpu.VMEM((rows, width), BF16),
            pltpu.VMEM((rows, width), BF16),
            pltpu.VMEM((3, width, columns), BF16),
            pltpu.VMEM((columns, width), BF16),
            pltpu.VMEM((4, 6, rows, HEAD_DIM), BF16),
            pltpu.VMEM((4, 2, patches, HEAD_DIM), BF16),
            pltpu.VMEM((2, 2, patches, HEAD_DIM), BF16),
            pltpu.VMEM((2, 12, patches, HEAD_DIM), BF16),
            pltpu.VMEM((2, n_seq, rows, block), BF16),
            pltpu.VMEM((2, 2, block, patches), BF16),
            pltpu.VMEM((2, 2, block, columns), F32),
            pltpu.VMEM(noise_value.shape, F32),
            pltpu.VMEM(noise_out.shape, F32),
            pltpu.VMEM((HEAD_DIM, patches), F32),
            pltpu.VMEM((n_seq, 16, HEAD_DIM), F32),
            pltpu.VMEM((n_ten, 16, HEAD_DIM), F32),
            dma((4,)),
            dma((4,)),
            dma((2,)),
            dma((4, n_seq)),
            dma((4, n_seq)),
            dma((2, n_seq)),
            dma((2, n_seq)),
            dma((2, n_seq, n_ten)),
            dma((2, n_seq, n_ten)),
            dma((2, 2, n_chip)),
            dma((2, 2, n_chip)),
            dma((2, 2, n_chip)),
            dma((2, 2, n_chip)),
            dma((n_seq,)),
            dma((n_seq,)),
            dma((n_ten,)),
            dma((n_ten,)),
        ],
        compiler_params=pltpu.CompilerParams(
            collective_id=0, has_side_effects=True, vmem_limit_bytes=60 * 1024 * 1024
        ),
    )(
        tokens.reshape(rows, width), cotangent.reshape(rows, width),
        w_query, w_key, w_value, w_out, noise_value, noise_out,
    )


def local(n_seq, n_ten, *arrays):
    images, patch, width = arrays[0].shape
    heads = arrays[1].shape[1] // HEAD_DIM
    fits = n_seq == 8 and n_ten == 4 and images == 2 and heads == 6 and patch == 128
    if fits and width == 3072:
        return local_fused(n_seq, n_ten, *arrays)
    return local_general(*arrays)


def solution(mesh):
    placed = (
        P(None, "seq", None),
        P(None, "tensor"),
        P(None, "tensor"),
        P(None, "tensor"),
        P("tensor", None),
        P(None, "seq", None),
        P("seq", "tensor"),
        P("tensor", "seq"),
    )
    return jax.shard_map(
        functools.partial(local, mesh.shape["seq"], mesh.shape["tensor"]),
        mesh=mesh,
        in_specs=placed,
        out_specs=(P("seq", "tensor"), P("tensor", "seq")),
        check_vma=False,
    )
```

```python
import functools
import math

import jax
import jax.numpy as jnp
from jax import lax
from jax.experimental import pallas as pl
from jax.experimental.pallas import tpu as pltpu
from jax.sharding import PartitionSpec as P

HEAD_DIM = 128


def local_general(tokens, w_query, w_key, w_value, w_out, cotangent, noise_value, noise_out):
    images, patch_rows, width = tokens.shape
    columns = w_query.shape[1]
    head_count = columns // HEAD_DIM
    score_scale = 1.0 / math.sqrt(HEAD_DIM)
    clip_bound = math.sqrt(2.0 * width * width)
    flat_tokens = tokens.reshape(images * patch_rows, width)

    token_columns = lax.all_to_all(tokens, "seq", split_axis=2, concat_axis=1, tiled=True)
    cot_columns = lax.all_to_all(cotangent, "seq", split_axis=2, concat_axis=1, tiled=True)

    def heads_first(rows):
        split = rows.reshape(images, patch_rows, head_count, HEAD_DIM)
        return split.transpose(0, 2, 1, 3)

    def project(weight):
        product = jnp.dot(flat_tokens, weight, preferred_element_type=jnp.float32)
        return product.astype(jnp.bfloat16)

    key_local = heads_first(project(w_key))
    keys_all = lax.all_gather(key_local, "seq", axis=2, tiled=True)
    value_local = heads_first(project(w_value))
    values_all = lax.all_gather(value_local, "seq", axis=2, tiled=True)
    queries = heads_first(project(w_query))
    flat_cotangent = cotangent.reshape(images * patch_rows, width)
    d_attn = jnp.einsum("rd,cd->rc", flat_cotangent, w_out, preferred_element_type=jnp.float32)
    d_attn = heads_first(d_attn.astype(jnp.bfloat16))
    scores = (
        jnp.einsum("ihqd,ihkd->ihqk", queries, keys_all, preferred_element_type=jnp.float32)
        * score_scale
    )
    row_totals = jax.nn.logsumexp(scores, axis=-1)
    attn_probs = jnp.exp(scores - row_totals[..., None]).astype(jnp.bfloat16)
    d_value = jnp.einsum(
        "ihqk,ihqd->ihkd", attn_probs, d_attn, preferred_element_type=jnp.float32
    ).astype(jnp.bfloat16)
    d_value = lax.psum_scatter(d_value, "seq", scatter_dimension=2, tiled=True)
    d_value_all = lax.all_gather(d_value, "seq", axis=2, tiled=True)
    attended = jnp.einsum(
        "ihqk,ihkd->ihqd", attn_probs, values_all, preferred_element_type=jnp.float32
    ).astype(jnp.bfloat16)
    attended_all = lax.all_gather(attended, "seq", axis=2, tiled=True)

    per_value = jnp.einsum(
        "ipe,ihpd->iehd", token_columns, d_value_all, preferred_element_type=jnp.float32
    ).reshape(images, -1, columns)
    per_out = jnp.einsum(
        "ihpd,ipe->ihde", attended_all, cot_columns, preferred_element_type=jnp.float32
    ).reshape(images, columns, -1)
    partial = jnp.sum(jnp.square(per_value), axis=(1, 2)) + jnp.sum(jnp.square(per_out), axis=(1, 2))
    squares = lax.psum(partial, ("seq", "tensor"))
    factor = clip_bound / (jnp.sqrt(squares) + 0.01)
    grad_value = noise_value
    grad_out = noise_out
    for image_index in range(images):
        grad_value = grad_value + factor[image_index] * per_value[image_index]
        grad_out = grad_out + factor[image_index] * per_out[image_index]
    return (grad_value / images, grad_out / images)


MESH = pl.DeviceIdType.MESH
F32 = jnp.float32
BF16 = jnp.bfloat16
ROWS_DOT = (((1,), (1,)), ((), ()))
DEPTH_DOT = (((0,), (0,)), ((), ()))


def fused_kernel(
    n_seq, n_ten, tok_h, cot_h, wq_h, wk_h, wv_h, wo_h, nv_h, no_h, gv, go,
    tok, cot, w3, wo, loc, recv, tmp, gath, cols, cols_t, acc, nv, no, probs, sq_seq, sq_ten,
    in_sem, w_sem, own_sem, a2a_s, a2a_r, hs_s, hs_r, tk_s, tk_r, fw_s, fw_r,
    ag_s, ag_r, sib_s, sib_r, sq_s, sq_r, st_s, st_r,
):
    me = lax.axis_index("seq")
    ten = lax.axis_index("tensor")
    chip, core = me // 2, me % 2
    n_chip = n_seq // 2
    sibling = 2 * chip + 1 - core
    rows = tok.shape[0]
    patch = rows // 2
    width = tok.shape[1]
    block = width // n_seq
    quarter = rows // n_ten
    patches = patch * n_seq
    half = patches // 2
    score_scale = 1.0 / math.sqrt(HEAD_DIM)

    loads = [
        pltpu.make_async_copy(tok_h, tok, in_sem.at[0]),
        pltpu.make_async_copy(wk_h, w3.at[0], w_sem.at[0]),
        pltpu.make_async_copy(wq_h, w3.at[1], w_sem.at[1]),
        pltpu.make_async_copy(wv_h, w3.at[2], w_sem.at[2]),
        pltpu.make_async_copy(cot_h, cot, in_sem.at[1]),
        pltpu.make_async_copy(wo_h, wo, w_sem.at[3]),
        pltpu.make_async_copy(nv_h, nv, in_sem.at[2]),
        pltpu.make_async_copy(no_h, no, in_sem.at[3]),
    ]
    for load in loads:
        load.start()

    barrier = pltpu.get_barrier_semaphore()
    for step in range(1, n_seq):
        pl.semaphore_signal(
            barrier, inc=1, device_id=((me + step) % n_seq, ten), device_id_type=MESH
        )
    for step in range(1, n_ten):
        pl.semaphore_signal(
            barrier, inc=1, device_id=(me, (ten + step) % n_ten), device_id_type=MESH
        )
    pl.semaphore_wait(barrier, n_seq + n_ten - 2)

    def remote(source, target, send_sem, recv_sem, seq_at, ten_at):
        return pltpu.make_async_remote_copy(
            src_ref=source, dst_ref=target, send_sem=send_sem, recv_sem=recv_sem,
            device_id=(seq_at, ten_at), device_id_type=MESH,
        )

    def head_rows(device):
        return pl.ds(pl.multiple_of(device * patch, patch), patch)

    def chip_heads(kind, at_chip):
        image = at_chip // 2
        return loc.at[
            kind, pl.ds(3 * (at_chip % 2), 3), pl.ds(pl.multiple_of(image * patch, patch), patch)
        ]

    def exchange(kind, step, source):
        other = (chip + step) % n_chip
        if source:
            other = (chip + n_chip - step) % n_chip
        peer = 2 * other + core
        return remote(
            chip_heads(kind, other), recv.at[kind, :, head_rows(peer if source else me)],
            a2a_s.at[kind, step], a2a_r.at[kind, step], peer, ten,
        )

    def pass_heads(kind, step, source):
        origin = 2 * ((chip + n_chip - step) % n_chip)
        to_core = core if source else 1 - core
        piece = recv.at[kind, pl.ds(to_core, 2), head_rows(origin + 1 - to_core)]
        return remote(
            piece, piece, hs_s.at[kind, step], hs_r.at[kind, step], sibling, ten
        )

    def send_heads(kind):
        @pl.loop(1, n_chip)
        def _(step):
            exchange(kind, step, False).start()

        recv[kind, :, head_rows(me), :] = loc[
            kind, pl.ds(3 * (chip % 2), 3),
            pl.ds(pl.multiple_of((chip // 2) * patch, patch), patch), :
        ]
        pass_heads(kind, 0, False).start()

    def pass_on(kind):
        @pl.loop(1, n_chip)
        def _(step):
            exchange(kind, step, True).wait_recv()
            pass_heads(kind, step, False).start()

    def have_heads(kind):
        @pl.loop(0, n_chip)
        def _(step):
            pass_heads(kind, step, True).wait_recv()

    def project(kind):
        @pl.loop(0, 3)
        def _(at):
            chunk = pl.ds(pl.multiple_of(at * 256, 256), 256)
            if kind < 3:
                out = jnp.dot(tok[...], w3[kind, :, chunk], preferred_element_type=F32)
            else:
                out = lax.dot_general(cot[...], wo[chunk, :], ROWS_DOT, preferred_element_type=F32)
            out = out.astype(BF16)
            loc[kind, 2 * at] = out[:, :HEAD_DIM]
            loc[kind, 2 * at + 1] = out[:, HEAD_DIM:]

    held = (tok, cot)

    def own_columns(which):
        return pltpu.make_async_copy(
            held[which].at[:, pl.ds(pl.multiple_of(me * block, block), block)],
            cols.at[which, me], own_sem.at[which],
        )

    def ten_rows(index):
        return pl.ds(pl.multiple_of(index * quarter, quarter), quarter)

    def column_copy(which, step, source):
        peer = (me + step) % n_seq
        if source:
            peer = (me + n_seq - step) % n_seq
        sender, target = (peer, me) if source else (me, peer)
        return remote(
            held[which].at[ten_rows(ten), pl.ds(pl.multiple_of(target * block, block), block)],
            cols.at[which, sender, ten_rows(ten), :],
            tk_s.at[which, step], tk_r.at[which, step], peer, ten,
        )

    def column_share(which, step, hop, source):
        origin = (me + n_seq - step) % n_seq
        peer = (ten + hop) % n_ten
        if source:
            peer = (ten + n_ten - hop) % n_ten
        piece = cols.at[which, origin, ten_rows(peer if source else ten), :]
        return remote(
            piece, piece, fw_s.at[which, step, hop], fw_r.at[which, step, hop], me, peer
        )

    def send_columns(which):
        own_columns(which).start()

        @pl.loop(1, n_seq)
        def _(step):
            column_copy(which, step, False).start()

    def share_columns(which):
        @pl.loop(1, n_seq)
        def _(step):
            column_copy(which, step, True).wait_recv()

            @pl.loop(1, n_ten)
            def _(hop):
                column_share(which, step, hop, False).start()

        own_columns(which).wait()

    loads[0].wait()
    send_columns(0)
    for kind in range(3):
        loads[1 + kind].wait()
        project(kind)
        send_heads(kind)
    loads[4].wait()
    loads[5].wait()
    project(3)
    send_heads(3)

    send_columns(1)
    pass_on(0)
    pass_on(1)
    have_heads(0)
    have_heads(1)
    blocks = patches // 256

    def strip(at):
        return pl.ds(pl.multiple_of(at * 256, 256), 256)

    @pl.loop(0, 2)
    def _(slot):
        @pl.loop(0, blocks)
        def _(at):
            scores = lax.dot_general(
                recv[1, core + slot, strip(at), :], recv[0, core + slot], ROWS_DOT,
                preferred_element_type=F32,
            ) * score_scale
            top = jnp.max(scores, axis=1, keepdims=True)
            raised = jnp.exp(scores - top)
            total = jnp.sum(raised, axis=1, keepdims=True)
            probs[slot, strip(at), :] = (raised * (1.0 / total)).astype(BF16)

    def own_head(at_chip, at_core):
        return (at_chip // 2) * 6 + 3 * (at_chip % 2) + 2 * at_core

    def shared_head(at_chip):
        return (at_chip // 2) * 6 + 3 * (at_chip % 2) + 1

    def half_rows(at_core):
        return pl.ds(pl.multiple_of(at_core * half, half), half)

    def place(which, part, at_chip, at_core):
        if part == 0:
            return gath.at[which, own_head(at_chip, at_core)]
        return gath.at[which, shared_head(at_chip), half_rows(at_core), :]

    def made(which, part):
        if part == 0:
            return tmp.at[which, core]
        return tmp.at[which, 1 - core, half_rows(core), :]

    def plane_copy(which, part, step, source):
        other = (chip + step) % n_chip
        if source:
            other = (chip + n_chip - step) % n_chip
        return remote(
            made(which, part), place(which, part, other if source else chip, core),
            ag_s.at[which, part, step], ag_r.at[which, part, step], 2 * other + core, ten,
        )

    def sibling_copy(which, part, step, source):
        origin = (chip + n_chip - step) % n_chip
        piece = place(which, part, origin, 1 - core if source else core)
        return remote(
            piece, piece, sib_s.at[which, part, step], sib_r.at[which, part, step], sibling, ten
        )

    def send_results(which):
        for part in range(2):
            @pl.loop(1, n_chip)
            def _(step):
                plane_copy(which, part, step, False).start()

        gath[which, own_head(chip, core)] = tmp[which, core]
        gath[which, shared_head(chip), half_rows(core), :] = tmp[
            which, 1 - core, half_rows(core), :
        ]
        for part in range(2):
            sibling_copy(which, part, 0, False).start()

    pass_on(2)
    have_heads(2)

    @pl.loop(0, 2)
    def _(slot):
        @pl.loop(0, blocks)
        def _(at):
            attended = jnp.dot(
                probs[slot, strip(at), :], recv[2, core + slot], preferred_element_type=F32
            )
            tmp[0, slot, strip(at), :] = attended.astype(BF16)

    send_results(0)
    pass_on(3)
    have_heads(3)

    @pl.loop(0, 2)
    def _(slot):
        @pl.loop(0, blocks)
        def _(at):
            d_value = lax.dot_general(
                recv[3, core + slot], probs[slot, :, strip(at)], DEPTH_DOT,
                preferred_element_type=F32,
            )
            tmp[1, slot, strip(at), :] = d_value.T.astype(BF16)

    send_results(1)
    share_columns(0)
    share_columns(1)

    def turn_columns(which):
        @pl.loop(1, n_seq)
        def _(step):
            @pl.loop(1, n_ten)
            def _(hop):
                column_share(which, step, hop, True).wait_recv()

        @pl.loop(0, n_seq)
        def _(origin):
            lanes = pl.ds(pl.multiple_of(origin * patch, patch), patch)
            for image in range(2):
                piece = cols[which, origin, image * patch:(image + 1) * patch, :]
                cols_t[which, image, :, lanes] = piece.T

    near = chip // 2
    partner = chip + 1 - 2 * (chip % 2)
    partner_step = (chip + n_chip - partner) % n_chip
    far_steps = [
        (chip + n_chip - (2 * (1 - near) + at)) % n_chip for at in range(2)
    ]

    def pass_results(which, step):
        for part in range(2):
            plane_copy(which, part, step, True).wait_recv()
            sibling_copy(which, part, step, False).start()

    def have_results(which, step):
        for part in range(2):
            sibling_copy(which, part, step, True).wait_recv()

    def multiply(which, image):
        @pl.loop(0, 3)
        def _(at):
            head = image * 6 + 2 * at
            heads = jnp.concatenate([gath[which, head], gath[which, head + 1]], axis=1)
            product = jnp.dot(cols_t[1 - which, image], heads, preferred_element_type=F32)
            acc[which, image, at] = product
            folded = jnp.sum((product * product).reshape(-1, 8, 256), axis=0)
            sq_seq[me, pl.ds(pl.multiple_of(image * 8, 8), 8), :] += (
                folded[:, :HEAD_DIM] + folded[:, HEAD_DIM:]
            )

    sq_seq[me] = jnp.zeros((16, HEAD_DIM), F32)
    pass_results(0, partner_step)
    turn_columns(1)
    pass_results(0, far_steps[0])
    pass_results(0, far_steps[1])
    pass_results(1, partner_step)
    turn_columns(0)
    have_results(0, 0)
    have_results(0, partner_step)
    multiply(0, near)
    have_results(0, far_steps[0])
    have_results(0, far_steps[1])
    multiply(0, 1 - near)
    have_results(1, 0)
    have_results(1, partner_step)
    multiply(1, near)
    pass_results(1, far_steps[0])
    pass_results(1, far_steps[1])
    have_results(1, far_steps[0])
    have_results(1, far_steps[1])
    multiply(1, 1 - near)

    def square_seq(step, source):
        peer = (me + step) % n_seq
        if source:
            peer = (me + n_seq - step) % n_seq
        piece = sq_seq.at[peer if source else me]
        return remote(piece, piece, sq_s.at[step], sq_r.at[step], peer, ten)

    def square_ten(step, source):
        peer = (ten + step) % n_ten
        if source:
            peer = (ten + n_ten - step) % n_ten
        piece = sq_ten.at[peer if source else ten]
        return remote(piece, piece, st_s.at[step], st_r.at[step], me, peer)

    for step in range(1, n_seq):
        square_seq(step, False).start()
    for step in range(1, n_seq):
        square_seq(step, True).wait_recv()
    sq_ten[ten] = jnp.sum(sq_seq[...], axis=0)
    for step in range(1, n_ten):
        square_ten(step, False).start()
    loads[6].wait()
    loads[7].wait()
    for step in range(1, n_ten):
        square_ten(step, True).wait_recv()
    total = jnp.sum(sq_ten[...], axis=0)
    norm = jnp.sum(jnp.sum(total.reshape(2, 8, HEAD_DIM), axis=1), axis=1, keepdims=True)
    factor = math.sqrt(2.0 * width * width) / (jnp.sqrt(norm) + 0.01)
    first, second = factor[0:1, :], factor[1:2, :]

    @pl.loop(0, 3)
    def _(at):
        lanes = strip(at)
        value = nv[:, lanes] + first * acc[1, 0, at] + second * acc[1, 1, at]
        gv[:, lanes] = value * 0.5
        mixed = first * acc[0, 0, at] + second * acc[0, 1, at]
        go[lanes, :] = (no[lanes, :] + mixed.T) * 0.5

    for kind in range(4):
        @pl.loop(1, n_chip)
        def _(step):
            exchange(kind, step, False).wait_send()

        @pl.loop(0, n_chip)
        def _(step):
            pass_heads(kind, step, False).wait_send()
    for which in range(2):
        @pl.loop(1, n_seq)
        def _(step):
            column_copy(which, step, False).wait_send()

            @pl.loop(1, n_ten)
            def _(hop):
                column_share(which, step, hop, False).wait_send()

        for part in range(2):
            @pl.loop(1, n_chip)
            def _(step):
                plane_copy(which, part, step, False).wait_send()

            @pl.loop(0, n_chip)
            def _(step):
                sibling_copy(which, part, step, False).wait_send()
    for step in range(1, n_seq):
        square_seq(step, False).wait_send()
    for step in range(1, n_ten):
        square_ten(step, False).wait_send()


def local_fused(
    n_seq, n_ten, tokens, w_query, w_key, w_value, w_out, cotangent, noise_value, noise_out
):
    images, patch, width = tokens.shape
    columns = w_query.shape[1]
    rows, patches, block = images * patch, patch * n_seq, width // n_seq
    n_chip = n_seq // 2
    dma = pltpu.SemaphoreType.DMA
    return pl.pallas_call(
        functools.partial(fused_kernel, n_seq, n_ten),
        out_shape=(
            jax.ShapeDtypeStruct(noise_value.shape, F32),
            jax.ShapeDtypeStruct(noise_out.shape, F32),
        ),
        in_specs=[pl.BlockSpec(memory_space=pl.ANY)] * 8,
        out_specs=[pl.BlockSpec(memory_space=pltpu.VMEM)] * 2,
        scratch_shapes=[
            pltpu.VMEM((rows, width), BF16),
            pltpu.VMEM((rows, width), BF16),
            pltpu.VMEM((3, width, columns), BF16),
            pltpu.VMEM((columns, width), BF16),
            pltpu.VMEM((4, 6, rows, HEAD_DIM), BF16),
            pltpu.VMEM((4, 3, patches, HEAD_DIM), BF16),
            pltpu.VMEM((2, 2, patches, HEAD_DIM), BF16),
            pltpu.VMEM((2, 12, patches, HEAD_DIM), BF16),
            pltpu.VMEM((2, n_seq, rows, block), BF16),
            pltpu.VMEM((2, 2, block, patches), BF16),
            pltpu.VMEM((2, 2, 3, block, 256), F32),
            pltpu.VMEM(noise_value.shape, F32),
            pltpu.VMEM(noise_out.shape, F32),
            pltpu.VMEM((2, patches, patches), BF16),
            pltpu.VMEM((n_seq, 16, HEAD_DIM), F32),
            pltpu.VMEM((n_ten, 16, HEAD_DIM), F32),
            dma((4,)),
            dma((4,)),
            dma((2,)),
            dma((4, n_chip)),
            dma((4, n_chip)),
            dma((4, n_chip)),
            dma((4, n_chip)),
            dma((2, n_seq)),
            dma((2, n_seq)),
            dma((2, n_seq, n_ten)),
            dma((2, n_seq, n_ten)),
            dma((2, 2, n_chip)),
            dma((2, 2, n_chip)),
            dma((2, 2, n_chip)),
            dma((2, 2, n_chip)),
            dma((n_seq,)),
            dma((n_seq,)),
            dma((n_ten,)),
            dma((n_ten,)),
        ],
        compiler_params=pltpu.CompilerParams(
            collective_id=0, has_side_effects=True, vmem_limit_bytes=60 * 1024 * 1024
        ),
    )(
        tokens.reshape(rows, width), cotangent.reshape(rows, width),
        w_query, w_key, w_value, w_out, noise_value, noise_out,
    )


def local(n_seq, n_ten, *arrays):
    images, patch, width = arrays[0].shape
    heads = arrays[1].shape[1] // HEAD_DIM
    fits = n_seq == 8 and n_ten == 4 and images == 2 and heads == 6 and patch == 128
    if fits and width == 3072:
        return local_fused(n_seq, n_ten, *arrays)
    return local_general(*arrays)


def solution(mesh):
    placed = (
        P(None, "seq", None),
        P(None, "tensor"),
        P(None, "tensor"),
        P(None, "tensor"),
        P("tensor", None),
        P(None, "seq", None),
        P("seq", "tensor"),
        P("tensor", "seq"),
    )
    return jax.shard_map(
        functools.partial(local, mesh.shape["seq"], mesh.shape["tensor"]),
        mesh=mesh,
        in_specs=placed,
        out_specs=(P("seq", "tensor"), P("tensor", "seq")),
        check_vma=False,
    )
```

```python
import functools
import math

import jax
import jax.numpy as jnp
from jax import lax
from jax.experimental import pallas as pl
from jax.experimental.pallas import tpu as pltpu
from jax.sharding import PartitionSpec as P

HEAD_DIM = 128


def local_general(tokens, w_query, w_key, w_value, w_out, cotangent, noise_value, noise_out):
    images, patch_rows, width = tokens.shape
    columns = w_query.shape[1]
    head_count = columns // HEAD_DIM
    score_scale = 1.0 / math.sqrt(HEAD_DIM)
    clip_bound = math.sqrt(2.0 * width * width)
    flat_tokens = tokens.reshape(images * patch_rows, width)

    token_columns = lax.all_to_all(tokens, "seq", split_axis=2, concat_axis=1, tiled=True)
    cot_columns = lax.all_to_all(cotangent, "seq", split_axis=2, concat_axis=1, tiled=True)

    def heads_first(rows):
        split = rows.reshape(images, patch_rows, head_count, HEAD_DIM)
        return split.transpose(0, 2, 1, 3)

    def project(weight):
        product = jnp.dot(flat_tokens, weight, preferred_element_type=jnp.float32)
        return product.astype(jnp.bfloat16)

    key_local = heads_first(project(w_key))
    keys_all = lax.all_gather(key_local, "seq", axis=2, tiled=True)
    value_local = heads_first(project(w_value))
    values_all = lax.all_gather(value_local, "seq", axis=2, tiled=True)
    queries = heads_first(project(w_query))
    flat_cotangent = cotangent.reshape(images * patch_rows, width)
    d_attn = jnp.einsum("rd,cd->rc", flat_cotangent, w_out, preferred_element_type=jnp.float32)
    d_attn = heads_first(d_attn.astype(jnp.bfloat16))
    scores = (
        jnp.einsum("ihqd,ihkd->ihqk", queries, keys_all, preferred_element_type=jnp.float32)
        * score_scale
    )
    row_totals = jax.nn.logsumexp(scores, axis=-1)
    attn_probs = jnp.exp(scores - row_totals[..., None]).astype(jnp.bfloat16)
    d_value = jnp.einsum(
        "ihqk,ihqd->ihkd", attn_probs, d_attn, preferred_element_type=jnp.float32
    ).astype(jnp.bfloat16)
    d_value = lax.psum_scatter(d_value, "seq", scatter_dimension=2, tiled=True)
    d_value_all = lax.all_gather(d_value, "seq", axis=2, tiled=True)
    attended = jnp.einsum(
        "ihqk,ihkd->ihqd", attn_probs, values_all, preferred_element_type=jnp.float32
    ).astype(jnp.bfloat16)
    attended_all = lax.all_gather(attended, "seq", axis=2, tiled=True)

    per_value = jnp.einsum(
        "ipe,ihpd->iehd", token_columns, d_value_all, preferred_element_type=jnp.float32
    ).reshape(images, -1, columns)
    per_out = jnp.einsum(
        "ihpd,ipe->ihde", attended_all, cot_columns, preferred_element_type=jnp.float32
    ).reshape(images, columns, -1)
    partial = jnp.sum(jnp.square(per_value), axis=(1, 2)) + jnp.sum(jnp.square(per_out), axis=(1, 2))
    squares = lax.psum(partial, ("seq", "tensor"))
    factor = clip_bound / (jnp.sqrt(squares) + 0.01)
    grad_value = noise_value
    grad_out = noise_out
    for image_index in range(images):
        grad_value = grad_value + factor[image_index] * per_value[image_index]
        grad_out = grad_out + factor[image_index] * per_out[image_index]
    return (grad_value / images, grad_out / images)


MESH = pl.DeviceIdType.MESH
F32 = jnp.float32
BF16 = jnp.bfloat16
ROWS_DOT = (((1,), (1,)), ((), ()))
DEPTH_DOT = (((0,), (0,)), ((), ()))


def fused_kernel(
    n_seq, n_ten, tok_h, cot_h, wk_h, wq_h, wv_h, wo_h, made_v, made_o, factor_out,
    tok, cot, w3, wo, loc, recv, tmp, gath, cols, cols_t, acc_v, acc_o, probs, sq_seq, sq_ten,
    in_sem, w_sem, own_sem, out_sem, a2a_s, a2a_r, hs_s, hs_r, tk_s, tk_r, fw_s, fw_r,
    ag_s, ag_r, sib_s, sib_r, sq_s, sq_r, st_s, st_r,
):
    me = lax.axis_index("seq")
    ten = lax.axis_index("tensor")
    chip, core = me // 2, me % 2
    n_chip = n_seq // 2
    sibling = 2 * chip + 1 - core
    rows = tok.shape[0]
    patch = rows // 2
    width = tok.shape[1]
    block = width // n_seq
    quarter = rows // n_ten
    patches = patch * n_seq
    half = patches // 2
    score_scale = 1.0 / math.sqrt(HEAD_DIM)

    loads = [
        pltpu.make_async_copy(tok_h, tok, in_sem.at[0]),
        pltpu.make_async_copy(wk_h, w3.at[0], w_sem.at[0]),
        pltpu.make_async_copy(wq_h, w3.at[1], w_sem.at[1]),
        pltpu.make_async_copy(wv_h, w3.at[2], w_sem.at[2]),
        pltpu.make_async_copy(cot_h, cot, in_sem.at[1]),
        pltpu.make_async_copy(wo_h, wo, w_sem.at[3]),
    ]
    for load in loads:
        load.start()

    barrier = pltpu.get_barrier_semaphore()
    for step in range(1, n_seq):
        pl.semaphore_signal(
            barrier, inc=1, device_id=((me + step) % n_seq, ten), device_id_type=MESH
        )
    for step in range(1, n_ten):
        pl.semaphore_signal(
            barrier, inc=1, device_id=(me, (ten + step) % n_ten), device_id_type=MESH
        )
    pl.semaphore_wait(barrier, n_seq + n_ten - 2)

    def remote(source, target, send_sem, recv_sem, seq_at, ten_at):
        return pltpu.make_async_remote_copy(
            src_ref=source, dst_ref=target, send_sem=send_sem, recv_sem=recv_sem,
            device_id=(seq_at, ten_at), device_id_type=MESH,
        )

    def head_rows(device):
        return pl.ds(pl.multiple_of(device * patch, patch), patch)

    def chip_heads(kind, at_chip):
        image = at_chip // 2
        return loc.at[
            kind, pl.ds(3 * (at_chip % 2), 3), pl.ds(pl.multiple_of(image * patch, patch), patch)
        ]

    def exchange(kind, step, source):
        other = (chip + step) % n_chip
        if source:
            other = (chip + n_chip - step) % n_chip
        peer = 2 * other + core
        return remote(
            chip_heads(kind, other), recv.at[kind, :, head_rows(peer if source else me)],
            a2a_s.at[kind, step], a2a_r.at[kind, step], peer, ten,
        )

    def pass_heads(kind, step, source):
        origin = 2 * ((chip + n_chip - step) % n_chip)
        to_core = core if source else 1 - core
        piece = recv.at[kind, pl.ds(to_core, 2), head_rows(origin + 1 - to_core)]
        return remote(
            piece, piece, hs_s.at[kind, step], hs_r.at[kind, step], sibling, ten
        )

    def send_heads(kind):
        @pl.loop(1, n_chip)
        def _(step):
            exchange(kind, step, False).start()

        recv[kind, :, head_rows(me), :] = loc[
            kind, pl.ds(3 * (chip % 2), 3),
            pl.ds(pl.multiple_of((chip // 2) * patch, patch), patch), :
        ]
        pass_heads(kind, 0, False).start()

    def pass_on(kind):
        @pl.loop(1, n_chip)
        def _(step):
            exchange(kind, step, True).wait_recv()
            pass_heads(kind, step, False).start()

    def have_heads(kind):
        @pl.loop(0, n_chip)
        def _(step):
            pass_heads(kind, step, True).wait_recv()

    def project(kind):
        @pl.loop(0, 3)
        def _(at):
            chunk = pl.ds(pl.multiple_of(at * 256, 256), 256)
            if kind < 3:
                out = jnp.dot(tok[...], w3[kind, :, chunk], preferred_element_type=F32)
            else:
                out = lax.dot_general(cot[...], wo[chunk, :], ROWS_DOT, preferred_element_type=F32)
            out = out.astype(BF16)
            loc[kind, 2 * at] = out[:, :HEAD_DIM]
            loc[kind, 2 * at + 1] = out[:, HEAD_DIM:]

    held = (tok, cot)

    def ten_rows(index):
        return pl.ds(pl.multiple_of(index * quarter, quarter), quarter)

    def own_columns(which):
        return pltpu.make_async_copy(
            held[which].at[ten_rows(ten), pl.ds(pl.multiple_of(me * block, block), block)],
            cols.at[which, me, ten_rows(ten), :], own_sem.at[which],
        )

    def column_copy(which, step, source):
        peer = (me + step) % n_seq
        if source:
            peer = (me + n_seq - step) % n_seq
        sender, target = (peer, me) if source else (me, peer)
        return remote(
            held[which].at[ten_rows(ten), pl.ds(pl.multiple_of(target * block, block), block)],
            cols.at[which, sender, ten_rows(ten), :],
            tk_s.at[which, step], tk_r.at[which, step], peer, ten,
        )

    def column_share(which, hop, source):
        peer = (ten + hop) % n_ten
        if source:
            peer = (ten + n_ten - hop) % n_ten
        piece = cols.at[which, :, ten_rows(peer if source else ten), :]
        return remote(piece, piece, fw_s.at[which, hop], fw_r.at[which, hop], me, peer)

    def send_columns(which):
        own_columns(which).start()

        @pl.loop(1, n_seq)
        def _(step):
            column_copy(which, step, False).start()

    def share_columns(which):
        @pl.loop(1, n_seq)
        def _(step):
            column_copy(which, step, True).wait_recv()

        own_columns(which).wait()

        @pl.loop(1, n_ten)
        def _(hop):
            column_share(which, hop, False).start()

    loads[0].wait()
    send_columns(0)
    loads[4].wait()
    send_columns(1)
    for kind in range(3):
        loads[1 + kind].wait()
        project(kind)
        send_heads(kind)
    loads[5].wait()
    project(3)
    send_heads(3)

    pass_on(0)
    share_columns(0)
    pass_on(1)
    share_columns(1)
    have_heads(0)
    have_heads(1)
    blocks = patches // 256

    def strip(at):
        return pl.ds(pl.multiple_of(at * 256, 256), 256)

    @pl.loop(0, 2)
    def _(slot):
        @pl.loop(0, blocks)
        def _(at):
            scores = lax.dot_general(
                recv[1, core + slot, strip(at), :], recv[0, core + slot], ROWS_DOT,
                preferred_element_type=F32,
            ) * score_scale
            top = jnp.max(scores, axis=1, keepdims=True)
            raised = jnp.exp(scores - top)
            total = jnp.sum(raised, axis=1, keepdims=True)
            probs[slot, strip(at), :] = (raised * (1.0 / total)).astype(BF16)

    def own_head(at_chip, at_core):
        return (at_chip // 2) * 6 + 3 * (at_chip % 2) + 2 * at_core

    def shared_head(at_chip):
        return (at_chip // 2) * 6 + 3 * (at_chip % 2) + 1

    def half_rows(at_core):
        return pl.ds(pl.multiple_of(at_core * half, half), half)

    def place(which, part, at_chip, at_core):
        if part == 0:
            return gath.at[which, own_head(at_chip, at_core)]
        return gath.at[which, shared_head(at_chip), half_rows(at_core), :]

    def made(which, part):
        if part == 0:
            return tmp.at[which, core]
        return tmp.at[which, 1 - core, half_rows(core), :]

    def plane_copy(which, part, step, source):
        other = (chip + step) % n_chip
        if source:
            other = (chip + n_chip - step) % n_chip
        return remote(
            made(which, part), place(which, part, other if source else chip, core),
            ag_s.at[which, part, step], ag_r.at[which, part, step], 2 * other + core, ten,
        )

    def sibling_copy(which, part, step, source):
        origin = (chip + n_chip - step) % n_chip
        piece = place(which, part, origin, 1 - core if source else core)
        return remote(
            piece, piece, sib_s.at[which, part, step], sib_r.at[which, part, step], sibling, ten
        )

    def send_results(which):
        for part in range(2):
            @pl.loop(1, n_chip)
            def _(step):
                plane_copy(which, part, step, False).start()

        gath[which, own_head(chip, core)] = tmp[which, core]
        gath[which, shared_head(chip), half_rows(core), :] = tmp[
            which, 1 - core, half_rows(core), :
        ]
        for part in range(2):
            sibling_copy(which, part, 0, False).start()

    pass_on(2)
    have_heads(2)

    @pl.loop(0, 2)
    def _(slot):
        @pl.loop(0, blocks)
        def _(at):
            attended = jnp.dot(
                probs[slot, strip(at), :], recv[2, core + slot], preferred_element_type=F32
            )
            tmp[0, slot, strip(at), :] = attended.astype(BF16)

    send_results(0)
    pass_on(3)
    have_heads(3)

    @pl.loop(0, 2)
    def _(slot):
        @pl.loop(0, blocks)
        def _(at):
            d_value = lax.dot_general(
                recv[3, core + slot], probs[slot, :, strip(at)], DEPTH_DOT,
                preferred_element_type=F32,
            )
            tmp[1, slot, strip(at), :] = d_value.T.astype(BF16)

    send_results(1)

    def turn_columns(which):
        @pl.loop(1, n_ten)
        def _(hop):
            column_share(which, hop, True).wait_recv()

        @pl.loop(0, n_seq)
        def _(origin):
            lanes = pl.ds(pl.multiple_of(origin * patch, patch), patch)
            for image in range(2):
                piece = cols[which, origin, image * patch:(image + 1) * patch, :]
                cols_t[which, image, :, lanes] = piece.T

    near = chip // 2
    partner = chip + 1 - 2 * (chip % 2)
    partner_step = (chip + n_chip - partner) % n_chip
    far_steps = [
        (chip + n_chip - (2 * (1 - near) + at)) % n_chip for at in range(2)
    ]

    def pass_results(which, step):
        for part in range(2):
            plane_copy(which, part, step, True).wait_recv()
            sibling_copy(which, part, step, False).start()

    def have_results(which, step):
        for part in range(2):
            sibling_copy(which, part, step, True).wait_recv()

    def hand_out(which, image):
        if which == 0:
            return pltpu.make_async_copy(acc_o.at[image], made_o.at[image], out_sem.at[0, image])
        return pltpu.make_async_copy(acc_v.at[image], made_v.at[image], out_sem.at[1, image])

    def multiply(which, image):
        @pl.loop(0, 3)
        def _(at):
            head = image * 6 + 2 * at
            heads = jnp.concatenate([gath[which, head], gath[which, head + 1]], axis=1)
            product = jnp.dot(cols_t[1 - which, image], heads, preferred_element_type=F32)
            if which == 0:
                acc_o[image, strip(at), :] = product.T
            else:
                acc_v[image, :, strip(at)] = product
            folded = jnp.sum((product * product).reshape(-1, 8, 256), axis=0)
            sq_seq[me, pl.ds(pl.multiple_of(image * 8, 8), 8), :] += (
                folded[:, :HEAD_DIM] + folded[:, HEAD_DIM:]
            )

        hand_out(which, image).start()

    def finish_early():
        for kind in range(4):
            @pl.loop(1, n_chip)
            def _(step):
                exchange(kind, step, False).wait_send()

            @pl.loop(0, n_chip)
            def _(step):
                pass_heads(kind, step, False).wait_send()

        for which in range(2):
            @pl.loop(1, n_seq)
            def _(step):
                column_copy(which, step, False).wait_send()

            @pl.loop(1, n_ten)
            def _(hop):
                column_share(which, hop, False).wait_send()

            for part in range(2):
                @pl.loop(1, n_chip)
                def _(step):
                    plane_copy(which, part, step, False).wait_send()

                @pl.loop(0, n_chip)
                def _(step):
                    sibling_copy(which, part, step, False).wait_send()

    sq_seq[me] = jnp.zeros((16, HEAD_DIM), F32)
    pass_results(0, partner_step)
    turn_columns(1)
    pass_results(0, far_steps[0])
    pass_results(0, far_steps[1])
    pass_results(1, partner_step)
    turn_columns(0)
    have_results(0, 0)
    have_results(0, partner_step)
    multiply(0, near)
    have_results(0, far_steps[0])
    have_results(0, far_steps[1])
    multiply(0, 1 - near)
    have_results(1, 0)
    have_results(1, partner_step)
    multiply(1, near)
    pass_results(1, far_steps[0])
    pass_results(1, far_steps[1])
    finish_early()
    have_results(1, far_steps[0])
    have_results(1, far_steps[1])
    multiply(1, 1 - near)

    def square_seq(step, source):
        peer = (me + step) % n_seq
        if source:
            peer = (me + n_seq - step) % n_seq
        piece = sq_seq.at[peer if source else me]
        return remote(piece, piece, sq_s.at[step], sq_r.at[step], peer, ten)

    def square_ten(step, source):
        peer = (ten + step) % n_ten
        if source:
            peer = (ten + n_ten - step) % n_ten
        piece = sq_ten.at[peer if source else ten]
        return remote(piece, piece, st_s.at[step], st_r.at[step], me, peer)

    for step in range(1, n_seq):
        square_seq(step, False).start()
    for step in range(1, n_seq):
        square_seq(step, True).wait_recv()
    sq_ten[ten] = jnp.sum(sq_seq[...], axis=0)
    for step in range(1, n_ten):
        square_ten(step, False).start()
    for step in range(1, n_ten):
        square_ten(step, True).wait_recv()
    total = jnp.sum(sq_ten[...], axis=0)
    norm = jnp.sum(jnp.sum(total.reshape(2, 8, HEAD_DIM), axis=1), axis=1, keepdims=True)
    factor = math.sqrt(2.0 * width * width) / (jnp.sqrt(norm) + 0.01)
    factor_out[...] = jnp.broadcast_to(factor, (2, HEAD_DIM))
    for which in range(2):
        for image in range(2):
            hand_out(which, image).wait()
    for step in range(1, n_seq):
        square_seq(step, False).wait_send()
    for step in range(1, n_ten):
        square_ten(step, False).wait_send()


def local_fused(
    n_seq, n_ten, tokens, w_query, w_key, w_value, w_out, cotangent, noise_value, noise_out
):
    images, patch, width = tokens.shape
    columns = w_query.shape[1]
    rows, patches, block = images * patch, patch * n_seq, width // n_seq
    n_chip = n_seq // 2
    dma = pltpu.SemaphoreType.DMA
    made_v, made_o, factor = pl.pallas_call(
        functools.partial(fused_kernel, n_seq, n_ten),
        out_shape=(
            jax.ShapeDtypeStruct((images, block, columns), F32),
            jax.ShapeDtypeStruct((images, columns, block), F32),
            jax.ShapeDtypeStruct((images, HEAD_DIM), F32),
        ),
        in_specs=[pl.BlockSpec(memory_space=pl.ANY)] * 6,
        out_specs=[
            pl.BlockSpec(memory_space=pl.ANY),
            pl.BlockSpec(memory_space=pl.ANY),
            pl.BlockSpec(memory_space=pltpu.VMEM),
        ],
        scratch_shapes=[
            pltpu.VMEM((rows, width), BF16),
            pltpu.VMEM((rows, width), BF16),
            pltpu.VMEM((3, width, columns), BF16),
            pltpu.VMEM((columns, width), BF16),
            pltpu.VMEM((4, 6, rows, HEAD_DIM), BF16),
            pltpu.VMEM((4, 3, patches, HEAD_DIM), BF16),
            pltpu.VMEM((2, 2, patches, HEAD_DIM), BF16),
            pltpu.VMEM((2, 12, patches, HEAD_DIM), BF16),
            pltpu.VMEM((2, n_seq, rows, block), BF16),
            pltpu.VMEM((2, 2, block, patches), BF16),
            pltpu.VMEM((images, block, columns), F32),
            pltpu.VMEM((images, columns, block), F32),
            pltpu.VMEM((2, patches, patches), BF16),
            pltpu.VMEM((n_seq, 16, HEAD_DIM), F32),
            pltpu.VMEM((n_ten, 16, HEAD_DIM), F32),
            dma((2,)),
            dma((4,)),
            dma((2,)),
            dma((2, 2)),
            dma((4, n_chip)),
            dma((4, n_chip)),
            dma((4, n_chip)),
            dma((4, n_chip)),
            dma((2, n_seq)),
            dma((2, n_seq)),
            dma((2, n_ten)),
            dma((2, n_ten)),
            dma((2, 2, n_chip)),
            dma((2, 2, n_chip)),
            dma((2, 2, n_chip)),
            dma((2, 2, n_chip)),
            dma((n_seq,)),
            dma((n_seq,)),
            dma((n_ten,)),
            dma((n_ten,)),
        ],
        compiler_params=pltpu.CompilerParams(
            collective_id=0, has_side_effects=True, vmem_limit_bytes=60 * 1024 * 1024
        ),
    )(
        tokens.reshape(rows, width), cotangent.reshape(rows, width),
        w_key, w_query, w_value, w_out,
    )
    first, second = factor[0, 0], factor[1, 0]
    return (
        (noise_value + first * made_v[0] + second * made_v[1]) * 0.5,
        (noise_out + first * made_o[0] + second * made_o[1]) * 0.5,
    )


def local(n_seq, n_ten, *arrays):
    images, patch, width = arrays[0].shape
    heads = arrays[1].shape[1] // HEAD_DIM
    fits = n_seq == 8 and n_ten == 4 and images == 2 and heads == 6 and patch == 128
    if fits and width == 3072:
        return local_fused(n_seq, n_ten, *arrays)
    return local_general(*arrays)


def solution(mesh):
    placed = (
        P(None, "seq", None),
        P(None, "tensor"),
        P(None, "tensor"),
        P(None, "tensor"),
        P("tensor", None),
        P(None, "seq", None),
        P("seq", "tensor"),
        P("tensor", "seq"),
    )
    return jax.shard_map(
        functools.partial(local, mesh.shape["seq"], mesh.shape["tensor"]),
        mesh=mesh,
        in_specs=placed,
        out_specs=(P("seq", "tensor"), P("tensor", "seq")),
        check_vma=False,
    )
```

```python
import functools
import math

import jax
import jax.numpy as jnp
from jax import lax
from jax.experimental import pallas as pl
from jax.experimental.pallas import tpu as pltpu
from jax.sharding import PartitionSpec as P

HEAD_DIM = 128


def local_general(tokens, w_query, w_key, w_value, w_out, cotangent, noise_value, noise_out):
    images, patch_rows, width = tokens.shape
    columns = w_query.shape[1]
    head_count = columns // HEAD_DIM
    score_scale = 1.0 / math.sqrt(HEAD_DIM)
    clip_bound = math.sqrt(2.0 * width * width)
    flat_tokens = tokens.reshape(images * patch_rows, width)

    token_columns = lax.all_to_all(tokens, "seq", split_axis=2, concat_axis=1, tiled=True)
    cot_columns = lax.all_to_all(cotangent, "seq", split_axis=2, concat_axis=1, tiled=True)

    def heads_first(rows):
        split = rows.reshape(images, patch_rows, head_count, HEAD_DIM)
        return split.transpose(0, 2, 1, 3)

    def project(weight):
        product = jnp.dot(flat_tokens, weight, preferred_element_type=jnp.float32)
        return product.astype(jnp.bfloat16)

    key_local = heads_first(project(w_key))
    keys_all = lax.all_gather(key_local, "seq", axis=2, tiled=True)
    value_local = heads_first(project(w_value))
    values_all = lax.all_gather(value_local, "seq", axis=2, tiled=True)
    queries = heads_first(project(w_query))
    flat_cotangent = cotangent.reshape(images * patch_rows, width)
    d_attn = jnp.einsum("rd,cd->rc", flat_cotangent, w_out, preferred_element_type=jnp.float32)
    d_attn = heads_first(d_attn.astype(jnp.bfloat16))
    scores = (
        jnp.einsum("ihqd,ihkd->ihqk", queries, keys_all, preferred_element_type=jnp.float32)
        * score_scale
    )
    row_totals = jax.nn.logsumexp(scores, axis=-1)
    attn_probs = jnp.exp(scores - row_totals[..., None]).astype(jnp.bfloat16)
    d_value = jnp.einsum(
        "ihqk,ihqd->ihkd", attn_probs, d_attn, preferred_element_type=jnp.float32
    ).astype(jnp.bfloat16)
    d_value = lax.psum_scatter(d_value, "seq", scatter_dimension=2, tiled=True)
    d_value_all = lax.all_gather(d_value, "seq", axis=2, tiled=True)
    attended = jnp.einsum(
        "ihqk,ihkd->ihqd", attn_probs, values_all, preferred_element_type=jnp.float32
    ).astype(jnp.bfloat16)
    attended_all = lax.all_gather(attended, "seq", axis=2, tiled=True)

    per_value = jnp.einsum(
        "ipe,ihpd->iehd", token_columns, d_value_all, preferred_element_type=jnp.float32
    ).reshape(images, -1, columns)
    per_out = jnp.einsum(
        "ihpd,ipe->ihde", attended_all, cot_columns, preferred_element_type=jnp.float32
    ).reshape(images, columns, -1)
    partial = jnp.sum(jnp.square(per_value), axis=(1, 2)) + jnp.sum(jnp.square(per_out), axis=(1, 2))
    squares = lax.psum(partial, ("seq", "tensor"))
    factor = clip_bound / (jnp.sqrt(squares) + 0.01)
    grad_value = noise_value
    grad_out = noise_out
    for image_index in range(images):
        grad_value = grad_value + factor[image_index] * per_value[image_index]
        grad_out = grad_out + factor[image_index] * per_out[image_index]
    return (grad_value / images, grad_out / images)


MESH = pl.DeviceIdType.MESH
F32 = jnp.float32
BF16 = jnp.bfloat16
ROWS_DOT = (((1,), (1,)), ((), ()))
DEPTH_DOT = (((0,), (0,)), ((), ()))


def fused_kernel(
    n_seq, n_ten, tok_h, cot_h, wk_h, wq_h, wv_h, wo_h, nv_h, no_h, gv, go,
    tok, cot, w3, wo, loc, recv, tmp, gath, cols, cols_t, acc_v, acc_o, nv, no, probs, sq_seq, sq_ten,
    in_sem, w_sem, own_sem, a2a_s, a2a_r, hs_s, hs_r, tk_s, tk_r, fw_s, fw_r,
    ag_s, ag_r, sib_s, sib_r, sq_s, sq_r, st_s, st_r,
):
    me = lax.axis_index("seq")
    ten = lax.axis_index("tensor")
    chip, core = me // 2, me % 2
    n_chip = n_seq // 2
    sibling = 2 * chip + 1 - core
    rows = tok.shape[0]
    patch = rows // 2
    width = tok.shape[1]
    block = width // n_seq
    quarter = rows // n_ten
    patches = patch * n_seq
    half = patches // 2
    score_scale = 1.0 / math.sqrt(HEAD_DIM)

    loads = [
        pltpu.make_async_copy(tok_h, tok, in_sem.at[0]),
        pltpu.make_async_copy(wk_h, w3.at[0], w_sem.at[0]),
        pltpu.make_async_copy(wq_h, w3.at[1], w_sem.at[1]),
        pltpu.make_async_copy(wv_h, w3.at[2], w_sem.at[2]),
        pltpu.make_async_copy(cot_h, cot, in_sem.at[1]),
        pltpu.make_async_copy(wo_h, wo, w_sem.at[3]),
        pltpu.make_async_copy(nv_h, nv, in_sem.at[2]),
        pltpu.make_async_copy(no_h, no, in_sem.at[3]),
    ]
    for load in loads:
        load.start()

    barrier = pltpu.get_barrier_semaphore()
    for step in range(1, n_seq):
        pl.semaphore_signal(
            barrier, inc=1, device_id=((me + step) % n_seq, ten), device_id_type=MESH
        )
    for step in range(1, n_ten):
        pl.semaphore_signal(
            barrier, inc=1, device_id=(me, (ten + step) % n_ten), device_id_type=MESH
        )
    pl.semaphore_wait(barrier, n_seq + n_ten - 2)

    def remote(source, target, send_sem, recv_sem, seq_at, ten_at):
        return pltpu.make_async_remote_copy(
            src_ref=source, dst_ref=target, send_sem=send_sem, recv_sem=recv_sem,
            device_id=(seq_at, ten_at), device_id_type=MESH,
        )

    def head_rows(device):
        return pl.ds(pl.multiple_of(device * patch, patch), patch)

    def chip_heads(kind, at_chip):
        image = at_chip // 2
        return loc.at[
            kind, pl.ds(3 * (at_chip % 2), 3), pl.ds(pl.multiple_of(image * patch, patch), patch)
        ]

    def exchange(kind, step, source):
        other = (chip + step) % n_chip
        if source:
            other = (chip + n_chip - step) % n_chip
        peer = 2 * other + core
        return remote(
            chip_heads(kind, other), recv.at[kind, :, head_rows(peer if source else me)],
            a2a_s.at[kind, step], a2a_r.at[kind, step], peer, ten,
        )

    def pass_heads(kind, step, source):
        origin = 2 * ((chip + n_chip - step) % n_chip)
        to_core = core if source else 1 - core
        piece = recv.at[kind, pl.ds(to_core, 2), head_rows(origin + 1 - to_core)]
        return remote(
            piece, piece, hs_s.at[kind, step], hs_r.at[kind, step], sibling, ten
        )

    def send_heads(kind):
        @pl.loop(1, n_chip)
        def _(step):
            exchange(kind, step, False).start()

        recv[kind, :, head_rows(me), :] = loc[
            kind, pl.ds(3 * (chip % 2), 3),
            pl.ds(pl.multiple_of((chip // 2) * patch, patch), patch), :
        ]
        pass_heads(kind, 0, False).start()

    def pass_on(kind):
        @pl.loop(1, n_chip)
        def _(step):
            exchange(kind, step, True).wait_recv()
            pass_heads(kind, step, False).start()

    def have_heads(kind):
        @pl.loop(0, n_chip)
        def _(step):
            pass_heads(kind, step, True).wait_recv()

    def project(kind):
        @pl.loop(0, 3)
        def _(at):
            chunk = pl.ds(pl.multiple_of(at * 256, 256), 256)
            if kind < 3:
                out = jnp.dot(tok[...], w3[kind, :, chunk], preferred_element_type=F32)
            else:
                out = lax.dot_general(cot[...], wo[chunk, :], ROWS_DOT, preferred_element_type=F32)
            out = out.astype(BF16)
            loc[kind, 2 * at] = out[:, :HEAD_DIM]
            loc[kind, 2 * at + 1] = out[:, HEAD_DIM:]

    held = (tok, cot)

    def ten_rows(index):
        return pl.ds(pl.multiple_of(index * quarter, quarter), quarter)

    def own_columns(which):
        return pltpu.make_async_copy(
            held[which].at[ten_rows(ten), pl.ds(pl.multiple_of(me * block, block), block)],
            cols.at[which, me, ten_rows(ten), :], own_sem.at[which],
        )

    def column_copy(which, step, source):
        peer = (me + step) % n_seq
        if source:
            peer = (me + n_seq - step) % n_seq
        sender, target = (peer, me) if source else (me, peer)
        return remote(
            held[which].at[ten_rows(ten), pl.ds(pl.multiple_of(target * block, block), block)],
            cols.at[which, sender, ten_rows(ten), :],
            tk_s.at[which, step], tk_r.at[which, step], peer, ten,
        )

    def column_share(which, hop, source):
        peer = (ten + hop) % n_ten
        if source:
            peer = (ten + n_ten - hop) % n_ten
        piece = cols.at[which, :, ten_rows(peer if source else ten), :]
        return remote(piece, piece, fw_s.at[which, hop], fw_r.at[which, hop], me, peer)

    def send_columns(which):
        own_columns(which).start()

        @pl.loop(1, n_seq)
        def _(step):
            column_copy(which, step, False).start()

    def share_columns(which):
        @pl.loop(1, n_seq)
        def _(step):
            column_copy(which, step, True).wait_recv()

        own_columns(which).wait()

        @pl.loop(1, n_ten)
        def _(hop):
            column_share(which, hop, False).start()

    loads[0].wait()
    send_columns(0)
    for kind in range(3):
        loads[1 + kind].wait()
        project(kind)
        send_heads(kind)
    loads[4].wait()
    loads[5].wait()
    project(3)
    send_heads(3)
    send_columns(1)

    pass_on(0)
    share_columns(0)
    pass_on(1)
    have_heads(0)
    have_heads(1)
    blocks = patches // 256

    def strip(at):
        return pl.ds(pl.multiple_of(at * 256, 256), 256)

    @pl.loop(0, 2)
    def _(slot):
        @pl.loop(0, blocks)
        def _(at):
            scores = lax.dot_general(
                recv[1, core + slot, strip(at), :], recv[0, core + slot], ROWS_DOT,
                preferred_element_type=F32,
            ) * score_scale
            top = jnp.max(scores, axis=1, keepdims=True)
            raised = jnp.exp(scores - top)
            total = jnp.sum(raised, axis=1, keepdims=True)
            probs[slot, strip(at), :] = (raised * (1.0 / total)).astype(BF16)

    def own_head(at_chip, at_core):
        return (at_chip // 2) * 6 + 3 * (at_chip % 2) + 2 * at_core

    def shared_head(at_chip):
        return (at_chip // 2) * 6 + 3 * (at_chip % 2) + 1

    def half_rows(at_core):
        return pl.ds(pl.multiple_of(at_core * half, half), half)

    def place(which, part, at_chip, at_core):
        if part == 0:
            return gath.at[which, own_head(at_chip, at_core)]
        return gath.at[which, shared_head(at_chip), half_rows(at_core), :]

    near = chip // 2
    partner = 4 * near + 1 - chip
    far_mid = 2 - near
    far_outer = 3 - 3 * near
    in_middle = (chip + near) % 2 == 1

    def block_copy(which, part, origin, to, slot):
        piece = place(which, part, origin, core)
        return remote(
            piece, piece, ag_s.at[which, part, slot], ag_r.at[which, part, origin],
            2 * to + core, ten,
        )

    def sibling_copy(which, part, origin, source):
        piece = place(which, part, origin, 1 - core if source else core)
        return remote(
            piece, piece, sib_s.at[which, part, origin], sib_r.at[which, part, origin],
            sibling, ten,
        )

    def send_results(which):
        gath[which, own_head(chip, core)] = tmp[which, core]
        gath[which, shared_head(chip), half_rows(core), :] = tmp[
            which, 1 - core, half_rows(core), :
        ]
        for part in range(2):
            block_copy(which, part, chip, far_mid, 1).start()
            block_copy(which, part, chip, partner, 0).start()
        for part in range(2):
            sibling_copy(which, part, chip, False).start()

    pass_on(2)
    have_heads(2)

    @pl.loop(0, 2)
    def _(slot):
        @pl.loop(0, blocks)
        def _(at):
            attended = jnp.dot(
                probs[slot, strip(at), :], recv[2, core + slot], preferred_element_type=F32
            )
            tmp[0, slot, strip(at), :] = attended.astype(BF16)

    send_results(0)
    pass_on(3)
    have_heads(3)

    @pl.loop(0, 2)
    def _(slot):
        @pl.loop(0, blocks)
        def _(at):
            d_value = lax.dot_general(
                recv[3, core + slot], probs[slot, :, strip(at)], DEPTH_DOT,
                preferred_element_type=F32,
            )
            tmp[1, slot, strip(at), :] = d_value.T.astype(BF16)

    send_results(1)
    share_columns(1)

    def turn_columns(which):
        @pl.loop(1, n_ten)
        def _(hop):
            column_share(which, hop, True).wait_recv()

        @pl.loop(0, n_seq)
        def _(origin):
            lanes = pl.ds(pl.multiple_of(origin * patch, patch), patch)
            for image in range(2):
                piece = cols[which, origin, image * patch:(image + 1) * patch, :]
                cols_t[which, image, :, lanes] = piece.T

    def pass_results(which, origin, slot):
        for part in range(2):
            block_copy(which, part, origin, partner, slot).wait_recv()
            if slot > 0:
                @pl.when(in_middle)
                def _():
                    block_copy(which, part, origin, partner, slot).start()
            sibling_copy(which, part, origin, False).start()

    def have_results(which, origin):
        for part in range(2):
            sibling_copy(which, part, origin, True).wait_recv()

    def multiply(which, image):
        @pl.loop(0, 3)
        def _(at):
            head = image * 6 + 2 * at
            heads = jnp.concatenate([gath[which, head], gath[which, head + 1]], axis=1)
            product = jnp.dot(cols_t[1 - which, image], heads, preferred_element_type=F32)
            if which == 0:
                acc_o[image, strip(at), :] = product.T
            else:
                acc_v[image, :, strip(at)] = product
            folded = jnp.sum((product * product).reshape(-1, 8, 256), axis=0)
            sq_seq[me, pl.ds(pl.multiple_of(image * 8, 8), 8), :] += (
                folded[:, :HEAD_DIM] + folded[:, HEAD_DIM:]
            )

    def finish_early():
        for kind in range(4):
            @pl.loop(1, n_chip)
            def _(step):
                exchange(kind, step, False).wait_send()

            @pl.loop(0, n_chip)
            def _(step):
                pass_heads(kind, step, False).wait_send()

        for which in range(2):
            @pl.loop(1, n_seq)
            def _(step):
                column_copy(which, step, False).wait_send()

            @pl.loop(1, n_ten)
            def _(hop):
                column_share(which, hop, False).wait_send()

            for part in range(2):
                block_copy(which, part, chip, partner, 0).wait_send()
                block_copy(which, part, chip, far_mid, 1).wait_send()

                @pl.when(in_middle)
                def _():
                    block_copy(which, part, far_mid, partner, 2).wait_send()
                    block_copy(which, part, far_outer, partner, 3).wait_send()

                @pl.loop(0, n_chip)
                def _(origin):
                    sibling_copy(which, part, origin, False).wait_send()

    sq_seq[me] = jnp.zeros((16, HEAD_DIM), F32)
    pass_results(0, partner, 0)
    pass_results(0, far_mid, 2)
    pass_results(0, far_outer, 3)
    turn_columns(0)
    pass_results(1, partner, 0)
    turn_columns(1)
    have_results(0, chip)
    have_results(0, partner)
    multiply(0, near)
    pass_results(1, far_mid, 2)
    have_results(0, far_mid)
    have_results(0, far_outer)
    multiply(0, 1 - near)
    pass_results(1, far_outer, 3)
    have_results(1, chip)
    have_results(1, partner)
    multiply(1, near)
    finish_early()
    have_results(1, far_mid)
    have_results(1, far_outer)
    multiply(1, 1 - near)

    def square_seq(step, source):
        peer = (me + step) % n_seq
        if source:
            peer = (me + n_seq - step) % n_seq
        piece = sq_seq.at[peer if source else me]
        return remote(piece, piece, sq_s.at[step], sq_r.at[step], peer, ten)

    def square_ten(step, source):
        peer = (ten + step) % n_ten
        if source:
            peer = (ten + n_ten - step) % n_ten
        piece = sq_ten.at[peer if source else ten]
        return remote(piece, piece, st_s.at[step], st_r.at[step], me, peer)

    for step in range(1, n_seq):
        square_seq(step, False).start()
    for step in range(1, n_seq):
        square_seq(step, True).wait_recv()
    sq_ten[ten] = jnp.sum(sq_seq[...], axis=0)
    for step in range(1, n_ten):
        square_ten(step, False).start()
    for step in range(1, n_ten):
        square_ten(step, True).wait_recv()
    total = jnp.sum(sq_ten[...], axis=0)
    norm = jnp.sum(jnp.sum(total.reshape(2, 8, HEAD_DIM), axis=1), axis=1, keepdims=True)
    factor = math.sqrt(2.0 * width * width) / (jnp.sqrt(norm) + 0.01)
    first, second = factor[0:1, :], factor[1:2, :]
    loads[6].wait()
    loads[7].wait()

    @pl.loop(0, 3)
    def _(at):
        lanes = strip(at)
        value = nv[:, lanes] + first * acc_v[0, :, lanes] + second * acc_v[1, :, lanes]
        gv[:, lanes] = value * 0.5
        value = no[lanes, :] + first * acc_o[0, lanes, :] + second * acc_o[1, lanes, :]
        go[lanes, :] = value * 0.5

    for step in range(1, n_seq):
        square_seq(step, False).wait_send()
    for step in range(1, n_ten):
        square_ten(step, False).wait_send()


def local_fused(
    n_seq, n_ten, tokens, w_query, w_key, w_value, w_out, cotangent, noise_value, noise_out
):
    images, patch, width = tokens.shape
    columns = w_query.shape[1]
    rows, patches, block = images * patch, patch * n_seq, width // n_seq
    n_chip = n_seq // 2
    dma = pltpu.SemaphoreType.DMA
    return pl.pallas_call(
        functools.partial(fused_kernel, n_seq, n_ten),
        out_shape=(
            jax.ShapeDtypeStruct(noise_value.shape, F32),
            jax.ShapeDtypeStruct(noise_out.shape, F32),
        ),
        in_specs=[pl.BlockSpec(memory_space=pl.ANY)] * 8,
        out_specs=[pl.BlockSpec(memory_space=pltpu.VMEM)] * 2,
        scratch_shapes=[
            pltpu.VMEM((rows, width), BF16),
            pltpu.VMEM((rows, width), BF16),
            pltpu.VMEM((3, width, columns), BF16),
            pltpu.VMEM((columns, width), BF16),
            pltpu.VMEM((4, 6, rows, HEAD_DIM), BF16),
            pltpu.VMEM((4, 3, patches, HEAD_DIM), BF16),
            pltpu.VMEM((2, 2, patches, HEAD_DIM), BF16),
            pltpu.VMEM((2, 12, patches, HEAD_DIM), BF16),
            pltpu.VMEM((2, n_seq, rows, block), BF16),
            pltpu.VMEM((2, 2, block, patches), BF16),
            pltpu.VMEM((images, block, columns), F32),
            pltpu.VMEM((images, columns, block), F32),
            pltpu.VMEM(noise_value.shape, F32),
            pltpu.VMEM(noise_out.shape, F32),
            pltpu.VMEM((2, patches, patches), BF16),
            pltpu.VMEM((n_seq, 16, HEAD_DIM), F32),
            pltpu.VMEM((n_ten, 16, HEAD_DIM), F32),
            dma((4,)),
            dma((4,)),
            dma((2,)),
            dma((4, n_chip)),
            dma((4, n_chip)),
            dma((4, n_chip)),
            dma((4, n_chip)),
            dma((2, n_seq)),
            dma((2, n_seq)),
            dma((2, n_ten)),
            dma((2, n_ten)),
            dma((2, 2, n_chip)),
            dma((2, 2, n_chip)),
            dma((2, 2, n_chip)),
            dma((2, 2, n_chip)),
            dma((n_seq,)),
            dma((n_seq,)),
            dma((n_ten,)),
            dma((n_ten,)),
        ],
        compiler_params=pltpu.CompilerParams(
            collective_id=0, has_side_effects=True, vmem_limit_bytes=60 * 1024 * 1024
        ),
    )(
        tokens.reshape(rows, width), cotangent.reshape(rows, width),
        w_key, w_query, w_value, w_out, noise_value, noise_out,
    )


def local(n_seq, n_ten, *arrays):
    images, patch, width = arrays[0].shape
    heads = arrays[1].shape[1] // HEAD_DIM
    fits = n_seq == 8 and n_ten == 4 and images == 2 and heads == 6 and patch == 128
    if fits and width == 3072:
        return local_fused(n_seq, n_ten, *arrays)
    return local_general(*arrays)


def solution(mesh):
    placed = (
        P(None, "seq", None),
        P(None, "tensor"),
        P(None, "tensor"),
        P(None, "tensor"),
        P("tensor", None),
        P(None, "seq", None),
        P("seq", "tensor"),
        P("tensor", "seq"),
    )
    return jax.shard_map(
        functools.partial(local, mesh.shape["seq"], mesh.shape["tensor"]),
        mesh=mesh,
        in_specs=placed,
        out_specs=(P("seq", "tensor"), P("tensor", "seq")),
        check_vma=False,
    )
```

```python
import functools
import math

import jax
import jax.numpy as jnp
from jax import lax
from jax.experimental import pallas as pl
from jax.experimental.pallas import tpu as pltpu
from jax.sharding import PartitionSpec as P

HEAD_DIM = 128


def local_general(tokens, w_query, w_key, w_value, w_out, cotangent, noise_value, noise_out):
    images, patch_rows, width = tokens.shape
    columns = w_query.shape[1]
    head_count = columns // HEAD_DIM
    score_scale = 1.0 / math.sqrt(HEAD_DIM)
    clip_bound = math.sqrt(2.0 * width * width)
    flat_tokens = tokens.reshape(images * patch_rows, width)

    token_columns = lax.all_to_all(tokens, "seq", split_axis=2, concat_axis=1, tiled=True)
    cot_columns = lax.all_to_all(cotangent, "seq", split_axis=2, concat_axis=1, tiled=True)

    def heads_first(rows):
        split = rows.reshape(images, patch_rows, head_count, HEAD_DIM)
        return split.transpose(0, 2, 1, 3)

    def project(weight):
        product = jnp.dot(flat_tokens, weight, preferred_element_type=jnp.float32)
        return product.astype(jnp.bfloat16)

    key_local = heads_first(project(w_key))
    keys_all = lax.all_gather(key_local, "seq", axis=2, tiled=True)
    value_local = heads_first(project(w_value))
    values_all = lax.all_gather(value_local, "seq", axis=2, tiled=True)
    queries = heads_first(project(w_query))
    flat_cotangent = cotangent.reshape(images * patch_rows, width)
    d_attn = jnp.einsum("rd,cd->rc", flat_cotangent, w_out, preferred_element_type=jnp.float32)
    d_attn = heads_first(d_attn.astype(jnp.bfloat16))
    scores = (
        jnp.einsum("ihqd,ihkd->ihqk", queries, keys_all, preferred_element_type=jnp.float32)
        * score_scale
    )
    row_totals = jax.nn.logsumexp(scores, axis=-1)
    attn_probs = jnp.exp(scores - row_totals[..., None]).astype(jnp.bfloat16)
    d_value = jnp.einsum(
        "ihqk,ihqd->ihkd", attn_probs, d_attn, preferred_element_type=jnp.float32
    ).astype(jnp.bfloat16)
    d_value = lax.psum_scatter(d_value, "seq", scatter_dimension=2, tiled=True)
    d_value_all = lax.all_gather(d_value, "seq", axis=2, tiled=True)
    attended = jnp.einsum(
        "ihqk,ihkd->ihqd", attn_probs, values_all, preferred_element_type=jnp.float32
    ).astype(jnp.bfloat16)
    attended_all = lax.all_gather(attended, "seq", axis=2, tiled=True)

    per_value = jnp.einsum(
        "ipe,ihpd->iehd", token_columns, d_value_all, preferred_element_type=jnp.float32
    ).reshape(images, -1, columns)
    per_out = jnp.einsum(
        "ihpd,ipe->ihde", attended_all, cot_columns, preferred_element_type=jnp.float32
    ).reshape(images, columns, -1)
    partial = jnp.sum(jnp.square(per_value), axis=(1, 2)) + jnp.sum(jnp.square(per_out), axis=(1, 2))
    squares = lax.psum(partial, ("seq", "tensor"))
    factor = clip_bound / (jnp.sqrt(squares) + 0.01)
    grad_value = noise_value
    grad_out = noise_out
    for image_index in range(images):
        grad_value = grad_value + factor[image_index] * per_value[image_index]
        grad_out = grad_out + factor[image_index] * per_out[image_index]
    return (grad_value / images, grad_out / images)


MESH = pl.DeviceIdType.MESH
F32 = jnp.float32
BF16 = jnp.bfloat16
ROWS_DOT = (((1,), (1,)), ((), ()))
DEPTH_DOT = (((0,), (0,)), ((), ()))


def fused_kernel(
    n_seq, n_ten, tok_h, cot_h, wk_h, wq_h, wv_h, wo_h, nv_h, no_h, gv, go,
    tok, cot, w3, wo, loc, recv, tmp, gath, cols, cols_t, acc_v, acc_o, nv, no, probs, sq_seq, sq_ten,
    in_sem, w_sem, own_sem, a2a_s, a2a_r, hs_s, hs_r, tk_s, tk_r, fw_s, fw_r,
    ag_s, ag_r, sib_s, sib_r, sq_s, sq_r, st_s, st_r,
):
    me = lax.axis_index("seq")
    ten = lax.axis_index("tensor")
    chip, core = me // 2, me % 2
    n_chip = n_seq // 2
    sibling = 2 * chip + 1 - core
    rows = tok.shape[0]
    patch = rows // 2
    width = tok.shape[1]
    block = width // n_seq
    quarter = rows // n_ten
    patches = patch * n_seq
    half = patches // 2
    score_scale = 1.0 / math.sqrt(HEAD_DIM)

    loads = [
        pltpu.make_async_copy(tok_h, tok, in_sem.at[0]),
        pltpu.make_async_copy(wk_h, w3.at[0], w_sem.at[0]),
        pltpu.make_async_copy(wq_h, w3.at[1], w_sem.at[1]),
        pltpu.make_async_copy(wv_h, w3.at[2], w_sem.at[2]),
        pltpu.make_async_copy(cot_h, cot, in_sem.at[1]),
        pltpu.make_async_copy(wo_h, wo, w_sem.at[3]),
        pltpu.make_async_copy(nv_h, nv, in_sem.at[2]),
        pltpu.make_async_copy(no_h, no, in_sem.at[3]),
    ]
    for load in loads:
        load.start()

    barrier = pltpu.get_barrier_semaphore()
    for step in range(1, n_seq):
        pl.semaphore_signal(
            barrier, inc=1, device_id=((me + step) % n_seq, ten), device_id_type=MESH
        )
    for step in range(1, n_ten):
        pl.semaphore_signal(
            barrier, inc=1, device_id=(me, (ten + step) % n_ten), device_id_type=MESH
        )
    pl.semaphore_wait(barrier, n_seq + n_ten - 2)

    def remote(source, target, send_sem, recv_sem, seq_at, ten_at):
        return pltpu.make_async_remote_copy(
            src_ref=source, dst_ref=target, send_sem=send_sem, recv_sem=recv_sem,
            device_id=(seq_at, ten_at), device_id_type=MESH,
        )

    def head_rows(device):
        return pl.ds(pl.multiple_of(device * patch, patch), patch)

    def chip_heads(kind, at_chip):
        image = at_chip // 2
        return loc.at[
            kind, pl.ds(3 * (at_chip % 2), 3), pl.ds(pl.multiple_of(image * patch, patch), patch)
        ]

    def exchange(kind, step, source):
        other = (chip + step) % n_chip
        if source:
            other = (chip + n_chip - step) % n_chip
        peer = 2 * other + core
        return remote(
            chip_heads(kind, other), recv.at[kind, :, head_rows(peer if source else me)],
            a2a_s.at[kind, step], a2a_r.at[kind, step], peer, ten,
        )

    def pass_heads(kind, step, source):
        origin = 2 * ((chip + n_chip - step) % n_chip)
        to_core = core if source else 1 - core
        piece = recv.at[kind, pl.ds(to_core, 2), head_rows(origin + 1 - to_core)]
        return remote(
            piece, piece, hs_s.at[kind, step], hs_r.at[kind, step], sibling, ten
        )

    def send_heads(kind):
        @pl.loop(1, n_chip)
        def _(step):
            exchange(kind, step, False).start()

        recv[kind, :, head_rows(me), :] = loc[
            kind, pl.ds(3 * (chip % 2), 3),
            pl.ds(pl.multiple_of((chip // 2) * patch, patch), patch), :
        ]
        pass_heads(kind, 0, False).start()

    def pass_on(kind):
        @pl.loop(1, n_chip)
        def _(step):
            exchange(kind, step, True).wait_recv()
            pass_heads(kind, step, False).start()

    def have_heads(kind):
        @pl.loop(0, n_chip)
        def _(step):
            pass_heads(kind, step, True).wait_recv()

    def project(kind):
        @pl.loop(0, 3)
        def _(at):
            chunk = pl.ds(pl.multiple_of(at * 256, 256), 256)
            if kind < 3:
                out = jnp.dot(tok[...], w3[kind, :, chunk], preferred_element_type=F32)
            else:
                out = lax.dot_general(cot[...], wo[chunk, :], ROWS_DOT, preferred_element_type=F32)
            out = out.astype(BF16)
            loc[kind, 2 * at] = out[:, :HEAD_DIM]
            loc[kind, 2 * at + 1] = out[:, HEAD_DIM:]

    held = (tok, cot)

    def ten_rows(index):
        return pl.ds(pl.multiple_of(index * quarter, quarter), quarter)

    def own_columns(which):
        return pltpu.make_async_copy(
            held[which].at[ten_rows(ten), pl.ds(pl.multiple_of(me * block, block), block)],
            cols.at[which, me, ten_rows(ten), :], own_sem.at[which],
        )

    def column_copy(which, step, source):
        peer = (me + step) % n_seq
        if source:
            peer = (me + n_seq - step) % n_seq
        sender, target = (peer, me) if source else (me, peer)
        return remote(
            held[which].at[ten_rows(ten), pl.ds(pl.multiple_of(target * block, block), block)],
            cols.at[which, sender, ten_rows(ten), :],
            tk_s.at[which, step], tk_r.at[which, step], peer, ten,
        )

    def column_share(which, hop, source):
        peer = (ten + hop) % n_ten
        if source:
            peer = (ten + n_ten - hop) % n_ten
        piece = cols.at[which, :, ten_rows(peer if source else ten), :]
        return remote(piece, piece, fw_s.at[which, hop], fw_r.at[which, hop], me, peer)

    def send_columns(which):
        own_columns(which).start()

        @pl.loop(1, n_seq)
        def _(step):
            column_copy(which, step, False).start()

    def share_columns(which):
        @pl.loop(1, n_seq)
        def _(step):
            column_copy(which, step, True).wait_recv()

        own_columns(which).wait()

        @pl.loop(1, n_ten)
        def _(hop):
            column_share(which, hop, False).start()

    loads[0].wait()
    send_columns(0)
    for kind in range(3):
        loads[1 + kind].wait()
        project(kind)
        send_heads(kind)
    loads[4].wait()
    loads[5].wait()
    project(3)
    send_heads(3)
    send_columns(1)

    pass_on(0)
    share_columns(0)
    pass_on(1)
    have_heads(0)
    have_heads(1)
    blocks = patches // 256

    def strip(at):
        return pl.ds(pl.multiple_of(at * 256, 256), 256)

    def score(slot):
        @pl.loop(0, blocks)
        def _(at):
            scores = lax.dot_general(
                recv[1, core + slot, strip(at), :], recv[0, core + slot], ROWS_DOT,
                preferred_element_type=F32,
            ) * score_scale
            top = jnp.max(scores, axis=1, keepdims=True)
            raised = jnp.exp(scores - top)
            total = jnp.sum(raised, axis=1, keepdims=True)
            probs[slot, strip(at), :] = (raised * (1.0 / total)).astype(BF16)

    def attend(slot):
        @pl.loop(0, blocks)
        def _(at):
            attended = jnp.dot(
                probs[slot, strip(at), :], recv[2, core + slot], preferred_element_type=F32
            )
            tmp[0, slot, strip(at), :] = attended.astype(BF16)

    def pull_back(slot):
        d_value = lax.dot_general(
            recv[3, core + slot], probs[slot], DEPTH_DOT, preferred_element_type=F32
        )
        tmp[1, slot] = d_value.T.astype(BF16)

    def own_head(at_chip, at_core):
        return (at_chip // 2) * 6 + 3 * (at_chip % 2) + 2 * at_core

    def shared_head(at_chip):
        return (at_chip // 2) * 6 + 3 * (at_chip % 2) + 1

    def half_rows(at_core):
        return pl.ds(pl.multiple_of(at_core * half, half), half)

    def place(which, part, at_chip, at_core):
        if part == 0:
            return gath.at[which, own_head(at_chip, at_core)]
        return gath.at[which, shared_head(at_chip), half_rows(at_core), :]

    near = chip // 2
    partner = 4 * near + 1 - chip
    far_mid = 2 - near
    far_outer = 3 - 3 * near
    in_middle = (chip + near) % 2 == 1

    def block_copy(which, part, origin, to, slot):
        piece = place(which, part, origin, core)
        return remote(
            piece, piece, ag_s.at[which, part, slot], ag_r.at[which, part, origin],
            2 * to + core, ten,
        )

    def sibling_copy(which, part, origin, source):
        piece = place(which, part, origin, 1 - core if source else core)
        return remote(
            piece, piece, sib_s.at[which, part, origin], sib_r.at[which, part, origin],
            sibling, ten,
        )

    def send_part(which, part):
        if part == 0:
            gath[which, own_head(chip, core)] = tmp[which, core]
        else:
            gath[which, shared_head(chip), half_rows(core), :] = tmp[
                which, 1 - core, half_rows(core), :
            ]
        block_copy(which, part, chip, far_mid, 1).start()
        block_copy(which, part, chip, partner, 0).start()
        sibling_copy(which, part, chip, False).start()

    score(core)
    pass_on(2)
    have_heads(2)
    attend(core)
    send_part(0, 0)
    score(1 - core)
    attend(1 - core)
    send_part(0, 1)
    pass_on(3)
    have_heads(3)
    pull_back(core)
    send_part(1, 0)
    pull_back(1 - core)
    send_part(1, 1)
    share_columns(1)

    def turn_columns(which):
        @pl.loop(1, n_ten)
        def _(hop):
            column_share(which, hop, True).wait_recv()

        @pl.loop(0, n_seq)
        def _(origin):
            lanes = pl.ds(pl.multiple_of(origin * patch, patch), patch)
            for image in range(2):
                piece = cols[which, origin, image * patch:(image + 1) * patch, :]
                cols_t[which, image, :, lanes] = piece.T

    def pass_results(which, origin, slot):
        for part in range(2):
            block_copy(which, part, origin, partner, slot).wait_recv()
            if slot > 0:
                @pl.when(in_middle)
                def _():
                    block_copy(which, part, origin, partner, slot).start()
            sibling_copy(which, part, origin, False).start()

    def have_results(which, origin):
        for part in range(2):
            sibling_copy(which, part, origin, True).wait_recv()

    def multiply(which, image):
        @pl.loop(0, 3)
        def _(at):
            head = image * 6 + 2 * at
            heads = jnp.concatenate([gath[which, head], gath[which, head + 1]], axis=1)
            product = jnp.dot(cols_t[1 - which, image], heads, preferred_element_type=F32)
            if which == 0:
                acc_o[image, strip(at), :] = product.T
            else:
                acc_v[image, :, strip(at)] = product
            folded = jnp.sum((product * product).reshape(-1, 8, 256), axis=0)
            sq_seq[me, pl.ds(pl.multiple_of(image * 8, 8), 8), :] += (
                folded[:, :HEAD_DIM] + folded[:, HEAD_DIM:]
            )

    def finish_early():
        for kind in range(4):
            @pl.loop(1, n_chip)
            def _(step):
                exchange(kind, step, False).wait_send()

            @pl.loop(0, n_chip)
            def _(step):
                pass_heads(kind, step, False).wait_send()

        for which in range(2):
            @pl.loop(1, n_seq)
            def _(step):
                column_copy(which, step, False).wait_send()

            @pl.loop(1, n_ten)
            def _(hop):
                column_share(which, hop, False).wait_send()

            for part in range(2):
                block_copy(which, part, chip, partner, 0).wait_send()
                block_copy(which, part, chip, far_mid, 1).wait_send()

                @pl.when(in_middle)
                def _():
                    block_copy(which, part, far_mid, partner, 2).wait_send()
                    block_copy(which, part, far_outer, partner, 3).wait_send()

                @pl.loop(0, n_chip)
                def _(origin):
                    sibling_copy(which, part, origin, False).wait_send()

    sq_seq[me] = jnp.zeros((16, HEAD_DIM), F32)
    pass_results(0, partner, 0)
    pass_results(0, far_mid, 2)
    pass_results(0, far_outer, 3)
    turn_columns(0)
    pass_results(1, partner, 0)
    turn_columns(1)
    have_results(0, chip)
    have_results(0, partner)
    multiply(0, near)
    pass_results(1, far_mid, 2)
    have_results(0, far_mid)
    have_results(0, far_outer)
    multiply(0, 1 - near)
    pass_results(1, far_outer, 3)
    have_results(1, chip)
    have_results(1, partner)
    multiply(1, near)
    finish_early()
    have_results(1, far_mid)
    have_results(1, far_outer)
    multiply(1, 1 - near)

    def square_seq(step, source):
        peer = (me + step) % n_seq
        if source:
            peer = (me + n_seq - step) % n_seq
        piece = sq_seq.at[peer if source else me]
        return remote(piece, piece, sq_s.at[step], sq_r.at[step], peer, ten)

    def square_ten(step, source):
        peer = (ten + step) % n_ten
        if source:
            peer = (ten + n_ten - step) % n_ten
        piece = sq_ten.at[peer if source else ten]
        return remote(piece, piece, st_s.at[step], st_r.at[step], me, peer)

    for step in range(1, n_seq):
        square_seq(step, False).start()
    for step in range(1, n_seq):
        square_seq(step, True).wait_recv()
    sq_ten[ten] = jnp.sum(sq_seq[...], axis=0)
    for step in range(1, n_ten):
        square_ten(step, False).start()
    for step in range(1, n_ten):
        square_ten(step, True).wait_recv()
    total = jnp.sum(sq_ten[...], axis=0)
    norm = jnp.sum(jnp.sum(total.reshape(2, 8, HEAD_DIM), axis=1), axis=1, keepdims=True)
    factor = math.sqrt(2.0 * width * width) / (jnp.sqrt(norm) + 0.01)
    first, second = factor[0:1, :], factor[1:2, :]
    loads[6].wait()
    loads[7].wait()

    @pl.loop(0, 3)
    def _(at):
        lanes = strip(at)
        value = nv[:, lanes] + first * acc_v[0, :, lanes] + second * acc_v[1, :, lanes]
        gv[:, lanes] = value * 0.5
        value = no[lanes, :] + first * acc_o[0, lanes, :] + second * acc_o[1, lanes, :]
        go[lanes, :] = value * 0.5

    for step in range(1, n_seq):
        square_seq(step, False).wait_send()
    for step in range(1, n_ten):
        square_ten(step, False).wait_send()


def local_fused(
    n_seq, n_ten, tokens, w_query, w_key, w_value, w_out, cotangent, noise_value, noise_out
):
    images, patch, width = tokens.shape
    columns = w_query.shape[1]
    rows, patches, block = images * patch, patch * n_seq, width // n_seq
    n_chip = n_seq // 2
    dma = pltpu.SemaphoreType.DMA
    return pl.pallas_call(
        functools.partial(fused_kernel, n_seq, n_ten),
        out_shape=(
            jax.ShapeDtypeStruct(noise_value.shape, F32),
            jax.ShapeDtypeStruct(noise_out.shape, F32),
        ),
        in_specs=[pl.BlockSpec(memory_space=pl.ANY)] * 8,
        out_specs=[pl.BlockSpec(memory_space=pltpu.VMEM)] * 2,
        scratch_shapes=[
            pltpu.VMEM((rows, width), BF16),
            pltpu.VMEM((rows, width), BF16),
            pltpu.VMEM((3, width, columns), BF16),
            pltpu.VMEM((columns, width), BF16),
            pltpu.VMEM((4, 6, rows, HEAD_DIM), BF16),
            pltpu.VMEM((4, 3, patches, HEAD_DIM), BF16),
            pltpu.VMEM((2, 2, patches, HEAD_DIM), BF16),
            pltpu.VMEM((2, 12, patches, HEAD_DIM), BF16),
            pltpu.VMEM((2, n_seq, rows, block), BF16),
            pltpu.VMEM((2, 2, block, patches), BF16),
            pltpu.VMEM((images, block, columns), F32),
            pltpu.VMEM((images, columns, block), F32),
            pltpu.VMEM(noise_value.shape, F32),
            pltpu.VMEM(noise_out.shape, F32),
            pltpu.VMEM((2, patches, patches), BF16),
            pltpu.VMEM((n_seq, 16, HEAD_DIM), F32),
            pltpu.VMEM((n_ten, 16, HEAD_DIM), F32),
            dma((4,)),
            dma((4,)),
            dma((2,)),
            dma((4, n_chip)),
            dma((4, n_chip)),
            dma((4, n_chip)),
            dma((4, n_chip)),
            dma((2, n_seq)),
            dma((2, n_seq)),
            dma((2, n_ten)),
            dma((2, n_ten)),
            dma((2, 2, n_chip)),
            dma((2, 2, n_chip)),
            dma((2, 2, n_chip)),
            dma((2, 2, n_chip)),
            dma((n_seq,)),
            dma((n_seq,)),
            dma((n_ten,)),
            dma((n_ten,)),
        ],
        compiler_params=pltpu.CompilerParams(
            collective_id=0, has_side_effects=True, vmem_limit_bytes=60 * 1024 * 1024
        ),
    )(
        tokens.reshape(rows, width), cotangent.reshape(rows, width),
        w_key, w_query, w_value, w_out, noise_value, noise_out,
    )


def local(n_seq, n_ten, *arrays):
    images, patch, width = arrays[0].shape
    heads = arrays[1].shape[1] // HEAD_DIM
    fits = n_seq == 8 and n_ten == 4 and images == 2 and heads == 6 and patch == 128
    if fits and width == 3072:
        return local_fused(n_seq, n_ten, *arrays)
    return local_general(*arrays)


def solution(mesh):
    placed = (
        P(None, "seq", None),
        P(None, "tensor"),
        P(None, "tensor"),
        P(None, "tensor"),
        P("tensor", None),
        P(None, "seq", None),
        P("seq", "tensor"),
        P("tensor", "seq"),
    )
    return jax.shard_map(
        functools.partial(local, mesh.shape["seq"], mesh.shape["tensor"]),
        mesh=mesh,
        in_specs=placed,
        out_specs=(P("seq", "tensor"), P("tensor", "seq")),
        check_vma=False,
    )
```

```python
import functools
import math

import jax
import jax.numpy as jnp
from jax import lax
from jax.experimental import pallas as pl
from jax.experimental.pallas import tpu as pltpu
from jax.sharding import PartitionSpec as P

HEAD_DIM = 128


def local_general(tokens, w_query, w_key, w_value, w_out, cotangent, noise_value, noise_out):
    images, patch_rows, width = tokens.shape
    columns = w_query.shape[1]
    head_count = columns // HEAD_DIM
    score_scale = 1.0 / math.sqrt(HEAD_DIM)
    clip_bound = math.sqrt(2.0 * width * width)
    flat_tokens = tokens.reshape(images * patch_rows, width)

    token_columns = lax.all_to_all(tokens, "seq", split_axis=2, concat_axis=1, tiled=True)
    cot_columns = lax.all_to_all(cotangent, "seq", split_axis=2, concat_axis=1, tiled=True)

    def heads_first(rows):
        split = rows.reshape(images, patch_rows, head_count, HEAD_DIM)
        return split.transpose(0, 2, 1, 3)

    def project(weight):
        product = jnp.dot(flat_tokens, weight, preferred_element_type=jnp.float32)
        return product.astype(jnp.bfloat16)

    key_local = heads_first(project(w_key))
    keys_all = lax.all_gather(key_local, "seq", axis=2, tiled=True)
    value_local = heads_first(project(w_value))
    values_all = lax.all_gather(value_local, "seq", axis=2, tiled=True)
    queries = heads_first(project(w_query))
    flat_cotangent = cotangent.reshape(images * patch_rows, width)
    d_attn = jnp.einsum("rd,cd->rc", flat_cotangent, w_out, preferred_element_type=jnp.float32)
    d_attn = heads_first(d_attn.astype(jnp.bfloat16))
    scores = (
        jnp.einsum("ihqd,ihkd->ihqk", queries, keys_all, preferred_element_type=jnp.float32)
        * score_scale
    )
    row_totals = jax.nn.logsumexp(scores, axis=-1)
    attn_probs = jnp.exp(scores - row_totals[..., None]).astype(jnp.bfloat16)
    d_value = jnp.einsum(
        "ihqk,ihqd->ihkd", attn_probs, d_attn, preferred_element_type=jnp.float32
    ).astype(jnp.bfloat16)
    d_value = lax.psum_scatter(d_value, "seq", scatter_dimension=2, tiled=True)
    d_value_all = lax.all_gather(d_value, "seq", axis=2, tiled=True)
    attended = jnp.einsum(
        "ihqk,ihkd->ihqd", attn_probs, values_all, preferred_element_type=jnp.float32
    ).astype(jnp.bfloat16)
    attended_all = lax.all_gather(attended, "seq", axis=2, tiled=True)

    per_value = jnp.einsum(
        "ipe,ihpd->iehd", token_columns, d_value_all, preferred_element_type=jnp.float32
    ).reshape(images, -1, columns)
    per_out = jnp.einsum(
        "ihpd,ipe->ihde", attended_all, cot_columns, preferred_element_type=jnp.float32
    ).reshape(images, columns, -1)
    partial = jnp.sum(jnp.square(per_value), axis=(1, 2)) + jnp.sum(jnp.square(per_out), axis=(1, 2))
    squares = lax.psum(partial, ("seq", "tensor"))
    factor = clip_bound / (jnp.sqrt(squares) + 0.01)
    grad_value = noise_value
    grad_out = noise_out
    for image_index in range(images):
        grad_value = grad_value + factor[image_index] * per_value[image_index]
        grad_out = grad_out + factor[image_index] * per_out[image_index]
    return (grad_value / images, grad_out / images)


MESH = pl.DeviceIdType.MESH
F32 = jnp.float32
BF16 = jnp.bfloat16
ROWS_DOT = (((1,), (1,)), ((), ()))
DEPTH_DOT = (((0,), (0,)), ((), ()))


def fused_kernel(
    n_seq, n_ten, tok_h, cot_h, wk_h, wq_h, wv_h, wo_h, nv_h, no_h, gv, go,
    tok, cot, w3, wo, loc, recv, tmp, gath, cols, cols_t, acc_v, acc_o, nv, no, probs, sq_seq, sq_ten,
    in_sem, w_sem, own_sem, a2a_s, a2a_r, hs_s, hs_r, tk_s, tk_r, fw_s, fw_r,
    ag_s, ag_r, sib_s, sib_r, sq_s, sq_r, st_s, st_r,
):
    me = lax.axis_index("seq")
    ten = lax.axis_index("tensor")
    chip, core = me // 2, me % 2
    n_chip = n_seq // 2
    sibling = 2 * chip + 1 - core
    rows = tok.shape[0]
    patch = rows // 2
    width = tok.shape[1]
    block = width // n_seq
    quarter = rows // n_ten
    patches = patch * n_seq
    half = patches // 2
    score_scale = 1.0 / math.sqrt(HEAD_DIM)

    loads = [
        pltpu.make_async_copy(tok_h, tok, in_sem.at[0]),
        pltpu.make_async_copy(wk_h, w3.at[0], w_sem.at[0]),
        pltpu.make_async_copy(wq_h, w3.at[1], w_sem.at[1]),
        pltpu.make_async_copy(wv_h, w3.at[2], w_sem.at[2]),
        pltpu.make_async_copy(cot_h, cot, in_sem.at[1]),
        pltpu.make_async_copy(wo_h, wo, w_sem.at[3]),
        pltpu.make_async_copy(nv_h, nv, in_sem.at[2]),
        pltpu.make_async_copy(no_h, no, in_sem.at[3]),
    ]
    for load in loads:
        load.start()

    barrier = pltpu.get_barrier_semaphore()
    for step in range(1, n_seq):
        pl.semaphore_signal(
            barrier, inc=1, device_id=((me + step) % n_seq, ten), device_id_type=MESH
        )
    for step in range(1, n_ten):
        pl.semaphore_signal(
            barrier, inc=1, device_id=(me, (ten + step) % n_ten), device_id_type=MESH
        )
    pl.semaphore_wait(barrier, n_seq + n_ten - 2)

    def remote(source, target, send_sem, recv_sem, seq_at, ten_at):
        return pltpu.make_async_remote_copy(
            src_ref=source, dst_ref=target, send_sem=send_sem, recv_sem=recv_sem,
            device_id=(seq_at, ten_at), device_id_type=MESH,
        )

    def head_rows(device):
        return pl.ds(pl.multiple_of(device * patch, patch), patch)

    def chip_heads(kind, at_chip):
        image = at_chip // 2
        return loc.at[
            kind, pl.ds(3 * (at_chip % 2), 3), pl.ds(pl.multiple_of(image * patch, patch), patch)
        ]

    def exchange(kind, step, source):
        other = (chip + step) % n_chip
        if source:
            other = (chip + n_chip - step) % n_chip
        peer = 2 * other + core
        return remote(
            chip_heads(kind, other), recv.at[kind, :, head_rows(peer if source else me)],
            a2a_s.at[kind, step], a2a_r.at[kind, step], peer, ten,
        )

    def pass_heads(kind, step, source):
        origin = 2 * ((chip + n_chip - step) % n_chip)
        to_core = core if source else 1 - core
        piece = recv.at[kind, pl.ds(to_core, 2), head_rows(origin + 1 - to_core)]
        return remote(
            piece, piece, hs_s.at[kind, step], hs_r.at[kind, step], sibling, ten
        )

    def send_heads(kind):
        @pl.loop(1, n_chip)
        def _(step):
            exchange(kind, step, False).start()

        recv[kind, :, head_rows(me), :] = loc[
            kind, pl.ds(3 * (chip % 2), 3),
            pl.ds(pl.multiple_of((chip // 2) * patch, patch), patch), :
        ]
        pass_heads(kind, 0, False).start()

    def pass_on(kind):
        @pl.loop(1, n_chip)
        def _(step):
            exchange(kind, step, True).wait_recv()
            pass_heads(kind, step, False).start()

    def have_heads(kind):
        @pl.loop(0, n_chip)
        def _(step):
            pass_heads(kind, step, True).wait_recv()

    def project(kind):
        @pl.loop(0, 3)
        def _(at):
            chunk = pl.ds(pl.multiple_of(at * 256, 256), 256)
            if kind < 3:
                out = jnp.dot(tok[...], w3[kind, :, chunk], preferred_element_type=F32)
            else:
                out = lax.dot_general(cot[...], wo[chunk, :], ROWS_DOT, preferred_element_type=F32)
            out = out.astype(BF16)
            loc[kind, 2 * at] = out[:, :HEAD_DIM]
            loc[kind, 2 * at + 1] = out[:, HEAD_DIM:]

    held = (tok, cot)

    def ten_rows(index):
        return pl.ds(pl.multiple_of(index * quarter, quarter), quarter)

    def own_columns(which):
        return pltpu.make_async_copy(
            held[which].at[ten_rows(ten), pl.ds(pl.multiple_of(me * block, block), block)],
            cols.at[which, me, ten_rows(ten), :], own_sem.at[which],
        )

    def column_copy(which, step, source):
        peer = (me + step) % n_seq
        if source:
            peer = (me + n_seq - step) % n_seq
        sender, target = (peer, me) if source else (me, peer)
        return remote(
            held[which].at[ten_rows(ten), pl.ds(pl.multiple_of(target * block, block), block)],
            cols.at[which, sender, ten_rows(ten), :],
            tk_s.at[which, step], tk_r.at[which, step], peer, ten,
        )

    def column_share(which, hop, source):
        peer = (ten + hop) % n_ten
        if source:
            peer = (ten + n_ten - hop) % n_ten
        piece = cols.at[which, :, ten_rows(peer if source else ten), :]
        return remote(piece, piece, fw_s.at[which, hop], fw_r.at[which, hop], me, peer)

    def send_columns(which):
        own_columns(which).start()

        @pl.loop(1, n_seq)
        def _(step):
            column_copy(which, step, False).start()

    def share_columns(which):
        @pl.loop(1, n_seq)
        def _(step):
            column_copy(which, step, True).wait_recv()

        own_columns(which).wait()

        @pl.loop(1, n_ten)
        def _(hop):
            column_share(which, hop, False).start()

    loads[0].wait()
    send_columns(0)
    for kind in range(3):
        loads[1 + kind].wait()
        project(kind)
        send_heads(kind)
    loads[4].wait()
    loads[5].wait()
    project(3)
    send_heads(3)
    send_columns(1)

    pass_on(0)
    share_columns(0)
    pass_on(1)
    have_heads(0)
    have_heads(1)
    blocks = patches // 256

    def strip(at):
        return pl.ds(pl.multiple_of(at * 256, 256), 256)

    def score(slot):
        @pl.loop(0, blocks)
        def _(at):
            scores = lax.dot_general(
                recv[1, core + slot, strip(at), :], recv[0, core + slot], ROWS_DOT,
                preferred_element_type=F32,
            ) * score_scale
            top = jnp.max(scores, axis=1, keepdims=True)
            raised = jnp.exp(scores - top)
            total = jnp.sum(raised, axis=1, keepdims=True)
            probs[slot, strip(at), :] = (raised * (1.0 / total)).astype(BF16)

    def attend(slot):
        @pl.loop(0, blocks)
        def _(at):
            attended = jnp.dot(
                probs[slot, strip(at), :], recv[2, core + slot], preferred_element_type=F32
            )
            tmp[0, slot, strip(at), :] = attended.astype(BF16)

    def pull_back(slot):
        d_value = lax.dot_general(
            recv[3, core + slot], probs[slot], DEPTH_DOT, preferred_element_type=F32
        )
        tmp[1, slot] = d_value.T.astype(BF16)

    def own_head(at_chip, at_core):
        return (at_chip // 2) * 6 + 3 * (at_chip % 2) + 2 * at_core

    def shared_head(at_chip):
        return (at_chip // 2) * 6 + 3 * (at_chip % 2) + 1

    def half_rows(at_core):
        return pl.ds(pl.multiple_of(at_core * half, half), half)

    def place(which, part, at_chip, at_core):
        if part == 0:
            return gath.at[which, own_head(at_chip, at_core)]
        return gath.at[which, shared_head(at_chip), half_rows(at_core), :]

    near = chip // 2
    partner = 4 * near + 1 - chip
    far_mid = 2 - near
    far_outer = 3 - 3 * near
    in_middle = (chip + near) % 2 == 1

    def block_copy(which, part, origin, to, slot):
        piece = place(which, part, origin, core)
        return remote(
            piece, piece, ag_s.at[which, part, slot], ag_r.at[which, part, origin],
            2 * to + core, ten,
        )

    def sibling_copy(which, part, origin, source):
        piece = place(which, part, origin, 1 - core if source else core)
        return remote(
            piece, piece, sib_s.at[which, part, origin], sib_r.at[which, part, origin],
            sibling, ten,
        )

    def send_part(which, part):
        if part == 0:
            gath[which, own_head(chip, core)] = tmp[which, core]
        else:
            gath[which, shared_head(chip), half_rows(core), :] = tmp[
                which, 1 - core, half_rows(core), :
            ]
        block_copy(which, part, chip, far_mid, 1).start()
        block_copy(which, part, chip, partner, 0).start()
        sibling_copy(which, part, chip, False).start()

    score(core)
    pass_on(2)
    have_heads(2)
    attend(core)
    send_part(0, 0)
    score(1 - core)
    attend(1 - core)
    send_part(0, 1)
    pass_on(3)
    have_heads(3)
    pull_back(core)
    send_part(1, 0)
    pull_back(1 - core)
    send_part(1, 1)
    share_columns(1)

    def turn_columns(which):
        @pl.loop(1, n_ten)
        def _(hop):
            column_share(which, hop, True).wait_recv()

        @pl.loop(0, n_seq)
        def _(origin):
            lanes = pl.ds(pl.multiple_of(origin * patch, patch), patch)
            for image in range(2):
                piece = cols[which, origin, image * patch:(image + 1) * patch, :]
                cols_t[which, image, :, lanes] = piece.T

    def pass_results(which, origin, slot, forward):
        for part in range(2):
            block_copy(which, part, origin, partner, slot).wait_recv()
            if forward:
                block_copy(which, part, origin, partner, slot).start()
            sibling_copy(which, part, origin, False).start()

    def have_results(which, origin):
        for part in range(2):
            sibling_copy(which, part, origin, True).wait_recv()

    def multiply(which, image):
        @pl.loop(0, 3)
        def _(at):
            head = image * 6 + 2 * at
            heads = jnp.concatenate([gath[which, head], gath[which, head + 1]], axis=1)
            product = jnp.dot(cols_t[1 - which, image], heads, preferred_element_type=F32)
            if which == 0:
                acc_o[image, strip(at), :] = product.T
            else:
                acc_v[image, :, strip(at)] = product
            folded = jnp.sum((product * product).reshape(-1, 8, 256), axis=0)
            sq_seq[me, pl.ds(pl.multiple_of(image * 8, 8), 8), :] += (
                folded[:, :HEAD_DIM] + folded[:, HEAD_DIM:]
            )

    def finish_early():
        for kind in range(4):
            @pl.loop(1, n_chip)
            def _(step):
                exchange(kind, step, False).wait_send()

            @pl.loop(0, n_chip)
            def _(step):
                pass_heads(kind, step, False).wait_send()

        for which in range(2):
            @pl.loop(1, n_seq)
            def _(step):
                column_copy(which, step, False).wait_send()

            @pl.loop(1, n_ten)
            def _(hop):
                column_share(which, hop, False).wait_send()

            for part in range(2):
                block_copy(which, part, chip, partner, 0).wait_send()
                block_copy(which, part, chip, far_mid, 1).wait_send()

                @pl.when(in_middle)
                def _():
                    block_copy(which, part, far_mid, partner, 2).wait_send()
                    block_copy(which, part, far_outer, partner, 3).wait_send()

                @pl.loop(0, n_chip)
                def _(origin):
                    sibling_copy(which, part, origin, False).wait_send()

    sq_seq[me] = jnp.zeros((16, HEAD_DIM), F32)
    def multiply_early():
        have_results(0, chip)
        have_results(0, partner)
        multiply(0, near)

    def multiply_late():
        have_results(0, far_mid)
        have_results(0, far_outer)
        multiply(0, 1 - near)

    @pl.when(in_middle)
    def _():
        pass_results(0, partner, 0, False)
        pass_results(0, far_mid, 2, True)
        pass_results(0, far_outer, 3, True)
        turn_columns(0)
        pass_results(1, partner, 0, False)
        pass_results(1, far_mid, 2, True)
        pass_results(1, far_outer, 3, True)
        turn_columns(1)
        multiply_early()
        multiply_late()

    @pl.when(jnp.logical_not(in_middle))
    def _():
        pass_results(0, partner, 0, False)
        turn_columns(0)
        pass_results(1, partner, 0, False)
        turn_columns(1)
        multiply_early()
        pass_results(0, far_mid, 2, False)
        pass_results(0, far_outer, 3, False)
        pass_results(1, far_mid, 2, False)
        multiply_late()
        pass_results(1, far_outer, 3, False)

    have_results(1, chip)
    have_results(1, partner)
    multiply(1, near)
    finish_early()
    have_results(1, far_mid)
    have_results(1, far_outer)
    multiply(1, 1 - near)

    def square_seq(step, source):
        peer = (me + step) % n_seq
        if source:
            peer = (me + n_seq - step) % n_seq
        piece = sq_seq.at[peer if source else me]
        return remote(piece, piece, sq_s.at[step], sq_r.at[step], peer, ten)

    def square_ten(step, source):
        peer = (ten + step) % n_ten
        if source:
            peer = (ten + n_ten - step) % n_ten
        piece = sq_ten.at[peer if source else ten]
        return remote(piece, piece, st_s.at[step], st_r.at[step], me, peer)

    for step in range(1, n_seq):
        square_seq(step, False).start()
    for step in range(1, n_seq):
        square_seq(step, True).wait_recv()
    sq_ten[ten] = jnp.sum(sq_seq[...], axis=0)
    for step in range(1, n_ten):
        square_ten(step, False).start()
    for step in range(1, n_ten):
        square_ten(step, True).wait_recv()
    total = jnp.sum(sq_ten[...], axis=0)
    norm = jnp.sum(jnp.sum(total.reshape(2, 8, HEAD_DIM), axis=1), axis=1, keepdims=True)
    factor = math.sqrt(2.0 * width * width) / (jnp.sqrt(norm) + 0.01)
    first, second = factor[0:1, :], factor[1:2, :]
    loads[6].wait()
    loads[7].wait()

    @pl.loop(0, 3)
    def _(at):
        lanes = strip(at)
        value = nv[:, lanes] + first * acc_v[0, :, lanes] + second * acc_v[1, :, lanes]
        gv[:, lanes] = value * 0.5
        value = no[lanes, :] + first * acc_o[0, lanes, :] + second * acc_o[1, lanes, :]
        go[lanes, :] = value * 0.5

    for step in range(1, n_seq):
        square_seq(step, False).wait_send()
    for step in range(1, n_ten):
        square_ten(step, False).wait_send()


def local_fused(
    n_seq, n_ten, tokens, w_query, w_key, w_value, w_out, cotangent, noise_value, noise_out
):
    images, patch, width = tokens.shape
    columns = w_query.shape[1]
    rows, patches, block = images * patch, patch * n_seq, width // n_seq
    n_chip = n_seq // 2
    dma = pltpu.SemaphoreType.DMA
    return pl.pallas_call(
        functools.partial(fused_kernel, n_seq, n_ten),
        out_shape=(
            jax.ShapeDtypeStruct(noise_value.shape, F32),
            jax.ShapeDtypeStruct(noise_out.shape, F32),
        ),
        in_specs=[pl.BlockSpec(memory_space=pl.ANY)] * 8,
        out_specs=[pl.BlockSpec(memory_space=pltpu.VMEM)] * 2,
        scratch_shapes=[
            pltpu.VMEM((rows, width), BF16),
            pltpu.VMEM((rows, width), BF16),
            pltpu.VMEM((3, width, columns), BF16),
            pltpu.VMEM((columns, width), BF16),
            pltpu.VMEM((4, 6, rows, HEAD_DIM), BF16),
            pltpu.VMEM((4, 3, patches, HEAD_DIM), BF16),
            pltpu.VMEM((2, 2, patches, HEAD_DIM), BF16),
            pltpu.VMEM((2, 12, patches, HEAD_DIM), BF16),
            pltpu.VMEM((2, n_seq, rows, block), BF16),
            pltpu.VMEM((2, 2, block, patches), BF16),
            pltpu.VMEM((images, block, columns), F32),
            pltpu.VMEM((images, columns, block), F32),
            pltpu.VMEM(noise_value.shape, F32),
            pltpu.VMEM(noise_out.shape, F32),
            pltpu.VMEM((2, patches, patches), BF16),
            pltpu.VMEM((n_seq, 16, HEAD_DIM), F32),
            pltpu.VMEM((n_ten, 16, HEAD_DIM), F32),
            dma((4,)),
            dma((4,)),
            dma((2,)),
            dma((4, n_chip)),
            dma((4, n_chip)),
            dma((4, n_chip)),
            dma((4, n_chip)),
            dma((2, n_seq)),
            dma((2, n_seq)),
            dma((2, n_ten)),
            dma((2, n_ten)),
            dma((2, 2, n_chip)),
            dma((2, 2, n_chip)),
            dma((2, 2, n_chip)),
            dma((2, 2, n_chip)),
            dma((n_seq,)),
            dma((n_seq,)),
            dma((n_ten,)),
            dma((n_ten,)),
        ],
        compiler_params=pltpu.CompilerParams(
            collective_id=0, has_side_effects=True, vmem_limit_bytes=60 * 1024 * 1024
        ),
    )(
        tokens.reshape(rows, width), cotangent.reshape(rows, width),
        w_key, w_query, w_value, w_out, noise_value, noise_out,
    )


def local(n_seq, n_ten, *arrays):
    images, patch, width = arrays[0].shape
    heads = arrays[1].shape[1] // HEAD_DIM
    fits = n_seq == 8 and n_ten == 4 and images == 2 and heads == 6 and patch == 128
    if fits and width == 3072:
        return local_fused(n_seq, n_ten, *arrays)
    return local_general(*arrays)


def solution(mesh):
    placed = (
        P(None, "seq", None),
        P(None, "tensor"),
        P(None, "tensor"),
        P(None, "tensor"),
        P("tensor", None),
        P(None, "seq", None),
        P("seq", "tensor"),
        P("tensor", "seq"),
    )
    return jax.shard_map(
        functools.partial(local, mesh.shape["seq"], mesh.shape["tensor"]),
        mesh=mesh,
        in_specs=placed,
        out_specs=(P("seq", "tensor"), P("tensor", "seq")),
        check_vma=False,
    )
```
